128 devices in a mesh: fsdp: 16 (over z, x_lo, core), tp: 8 (over y, x_hi).
Axes of the slice: x: 4 (x_hi: 2, x_lo: 2; x = x_hi * 2 + x_lo), y: 4, z: 4, core: 2. Of those that a mesh axis runs over, the one named last changes fastest.
Arguments:
- hidden_in: bfloat16 [2048, 4, 8192], P('fsdp'), may hold values from -6 to 6
- lengths: int32 [2048], P('fsdp'), may hold values from 1 to 128, as said below
- key_cache: bfloat16 [2048, 128, 1024], P('fsdp', None, 'tp'), may hold values from -400 to 400
- value_cache: bfloat16 [2048, 128, 1024], P('fsdp', None, 'tp'), may hold values from -6 to 6
- query_weight: bfloat16 [8192, 4096], P('fsdp'), may hold values from -0.0625 to 0.0625
- key_weight: bfloat16 [8192, 1024], P('fsdp'), may hold values from -0.0625 to 0.0625
- value_weight: bfloat16 [8192, 1024], P('fsdp'), may hold values from -0.0625 to 0.0625
- out_weight: bfloat16 [4096, 8192], P(None, 'fsdp'), may hold values from -0.5 to 0.5
Outputs:
- attn_out: bfloat16 [2048, 4, 8192], P('fsdp')
The draws below stay inside these ranges and needn't reach their ends.
Inputs may be any that keep to these rules, and one draw needn't show every extreme that they name: `lengths`: some row fills all 128 slots; slots at or beyond a row's length hold stale data.
All inputs are finite; a program needn't handle non-finite values.
Results may differ from the reference program's by a relative error of at most 0.012.
Values may be sent and summed in bfloat16 or wider, within the bound.
A program may use at most 192 MiB of HBM per device.

```python
import math
import jax
import jax.numpy as jnp
from jax import lax

D = 8192
HQ = 32
KVH = 8
HD = 128
STEPS = 4
CTX = 128
TOTAL_ROWS = 2048


def draw_lengths(key, part):
    key = jax.random.fold_in(key, 5)
    first_key, second_key = jax.random.split(key, 2)
    drawn_lengths = jax.random.randint(first_key, (TOTAL_ROWS,), 1, CTX + 1)
    chosen_row = jax.random.randint(second_key, (), 0, TOTAL_ROWS)
    return jnp.where(jnp.arange(TOTAL_ROWS, dtype=jnp.int32) == chosen_row, CTX, drawn_lengths).astype(jnp.int32)


def draw_key_cache(key, part):
    key = jax.random.fold_in(key, 11)
    base_key = jax.random.fold_in(key, 0)
    array_shape = (TOTAL_ROWS, CTX, KVH * HD)
    base_keys = jnp.clip(jax.random.normal(base_key, array_shape, jnp.float32), -6.0, 6.0)
    return base_keys.astype(jnp.bfloat16)


def block_scale(own_key, extent, shards, smallest, largest):
    level, own = 1.0, jax.random.fold_in(own_key, 6)
    for position, shards_of in shards:
        heights = jnp.exp(jax.random.uniform(jax.random.fold_in(own, position), (shards_of,), jnp.float32, smallest / len(shards), largest / len(shards)))
        level = level * jnp.repeat(heights, extent[position] // shards_of).reshape([-1 if axis == position else 1 for axis in range(len(extent))])
    return level


def centred(rng, shape, spread, bound, shards=(), held_as=jnp.bfloat16):
    loudness = block_scale(rng, shape, shards, -0.22, 0.18) if shards else 1.0
    values = jax.random.normal(rng, shape, jnp.float32) * spread * loudness
    return jnp.minimum(jnp.maximum(values, -bound), bound).astype(held_as)


def setup_inputs(seed: int = 0) -> dict:
    arg_keys = jax.random.split(jax.random.key(seed), 9)
    hidden_in = centred(arg_keys[0], (TOTAL_ROWS, STEPS, D), 1.0, 6.0, ((0, 16),))
    lengths = draw_lengths(jax.random.fold_in(arg_keys[8], 71), 0)
    key_cache = draw_key_cache(jax.random.fold_in(arg_keys[8], 71), 0)
    value_cache = centred(arg_keys[3], (TOTAL_ROWS, CTX, KVH * HD), 1.0, 6.0, ((0, 16), (2, 8)))
    query_weight = centred(arg_keys[4], (D, HQ * HD), D ** -0.5, 0.0625, ((0, 16),))
    key_weight = centred(arg_keys[5], (D, KVH * HD), D ** -0.5, 0.0625, ((0, 16),))
    value_weight = centred(arg_keys[6], (D, KVH * HD), D ** -0.5, 0.0625, ((0, 16),))
    out_weight = centred(arg_keys[7], (HQ * HD, D), HD ** -0.5, 0.5, ((1, 16),))
    return dict(hidden_in=hidden_in, lengths=lengths, key_cache=key_cache, value_cache=value_cache, query_weight=query_weight, key_weight=key_weight, value_weight=value_weight, out_weight=out_weight)


rope_base = 1000000.0
epsilon = 1e-06
masked = -1e+30

def rotate(values, positions):
    middle = values.shape[-1] // 2
    frequency = rope_base ** (-(jnp.arange(middle, dtype=jnp.float32) * 2.0) / values.shape[-1])
    angles = positions.astype(jnp.float32)[..., None] * frequency
    cosine = jnp.cos(angles)
    sine_part = jnp.sin(angles)
    former = values[..., :middle]
    latter = values[..., middle:]
    return jnp.concatenate([former * cosine - latter * sine_part, latter * cosine + former * sine_part], axis=-1)

def attend(queries, cached_keys, cached_values, fresh_keys, fresh_values, lengths):
    row_count, step_count, group_size, head_size = queries.shape
    slot_count = cached_keys.shape[1]
    scaling = 1.0 / math.sqrt(head_size)
    query_float = queries.astype(jnp.float32)
    older_scores = jnp.einsum('rsqd,rld->rsql', query_float, cached_keys.astype(jnp.float32)) * scaling
    recent = jnp.einsum('rsqd,rtd->rsqt', query_float, fresh_keys.astype(jnp.float32)) * scaling
    live_slots = jnp.arange(slot_count, dtype=jnp.int32)[None, :] < lengths[:, None]
    older_scores = jnp.where(live_slots[:, None, None, :], older_scores, masked)
    causal = jnp.arange(step_count, dtype=jnp.int32)[None, :] <= jnp.arange(step_count, dtype=jnp.int32)[:, None]
    recent = jnp.where(causal[None, :, None, :], recent, masked)
    highest = jnp.maximum(lax.optimization_barrier(jnp.max(older_scores, axis=-1)), lax.optimization_barrier(jnp.max(recent, axis=-1)))[..., None]
    older_exp = jnp.exp(older_scores - highest)
    recent_exp = jnp.exp(recent - highest)
    totals = lax.optimization_barrier(jnp.sum(older_exp, axis=-1, keepdims=True)) + lax.optimization_barrier(jnp.sum(recent_exp, axis=-1, keepdims=True))
    older_prob = (older_exp / totals).astype(jnp.bfloat16)
    recent_prob = (recent_exp / totals).astype(jnp.bfloat16)
    mixture = jnp.einsum('rsql,rld->rsqd', older_prob.astype(jnp.float32), cached_values.astype(jnp.float32))
    mixture = mixture + jnp.einsum('rsqt,rtd->rsqd', recent_prob.astype(jnp.float32), fresh_values.astype(jnp.float32))
    return mixture.astype(jnp.bfloat16)

def reference(hidden_in, lengths, key_cache, value_cache, query_weight, key_weight, value_weight, out_weight):
    row_count, step_count, model_width = hidden_in.shape
    token_count = row_count * step_count
    group_size = HQ // KVH
    flat_rows = hidden_in.astype(jnp.float32).reshape(token_count, model_width)
    normed = (flat_rows * lax.rsqrt(lax.optimization_barrier(jnp.mean(flat_rows * flat_rows, axis=1, keepdims=True)) + epsilon)).astype(jnp.bfloat16)
    queries = jnp.dot(normed, query_weight, preferred_element_type=jnp.float32)
    keys_raw = jnp.dot(normed, key_weight, preferred_element_type=jnp.float32)
    values_raw = jnp.dot(normed, value_weight, preferred_element_type=jnp.float32)
    positions = lengths[:, None] + jnp.arange(step_count, dtype=jnp.int32)[None, :]
    rotated_queries = rotate(queries.reshape(row_count, step_count, KVH, group_size, HD), positions[:, :, None, None]).astype(jnp.bfloat16)
    rotated_keys = rotate(keys_raw.reshape(row_count, step_count, KVH, HD), positions[:, :, None]).astype(jnp.bfloat16)
    new_values = values_raw.reshape(row_count, step_count, KVH, HD).astype(jnp.bfloat16)
    pieces = []
    for head_index in range(KVH):
        column_start = head_index * HD
        pieces.append(attend(rotated_queries[:, :, head_index], key_cache[:, :, column_start:column_start + HD], value_cache[:, :, column_start:column_start + HD], rotated_keys[:, :, head_index], new_values[:, :, head_index], lengths))
    context = jnp.stack(pieces, axis=2).reshape(token_count, HQ * HD)
    attn_out = jnp.dot(context, out_weight, preferred_element_type=jnp.float32).astype(jnp.bfloat16)
    return attn_out.reshape(row_count, step_count, model_width)
```

```python
import functools
import math

import jax
import jax.numpy as jnp
from jax import lax
from jax.experimental import pallas as pl
from jax.experimental.pallas import tpu as pltpu
from jax.sharding import PartitionSpec as P

HD = 128
STEPS = 4
GROUP = 4
LANES = 128
rope_base = 1000000.0
epsilon = 1e-06
masked = -1e30

MESH = pl.DeviceIdType.MESH
f32 = jnp.float32
bf16 = jnp.bfloat16

PROJ_JOBS = 6
OUT_JOBS = 4
JOBS = PROJ_JOBS + OUT_JOBS
BLOCK = 512
TOKENS = 512
CHUNKS = 4
CHUNK = TOKENS // CHUNKS
UNITS = 8
TP = 8
SENDS = 15


def al(x, m):
    return pl.multiple_of(x, m)


def layer_kernel(
    hidden, kcache, vcache, wq, wk, wv, wo, cos_ref, sin_ref, len_ref,
    out,
    wbuf, xn, kc, vc, qr, kn, vn, ctx, obuf, acc,
    gsend, grecv, csend, crecv, osend, orecv, local_sem,
):
    f, t = lax.axis_index("fsdp"), lax.axis_index("tp")
    z, lo, c = f // 4, (f // 2) % 2, f % 2
    y, hi = t // 2, t % 2
    c_is_hi = c == hi

    def dev(zz=z, ll=lo, cc=c, yy=y, hh=hi):
        return (zz * 4 + ll * 2 + cc, yy * 2 + hh)

    zp, zm = (z + 1) % 4, (z + 3) % 4
    yp, ym = (y + 1) % 4, (y + 3) % 4
    d_zp, d_zm = dev(zz=zp), dev(zz=zm)
    d_yp, d_ym = dev(yy=yp), dev(yy=ym)
    d_pair, d_hi, d_sib = dev(ll=1 - lo), dev(hh=1 - hi), dev(cc=1 - c)
    d_cross = dev(ll=1 - lo, hh=1 - hi)
    d_cross_sib = dev(ll=1 - lo, hh=1 - hi, cc=1 - c)

    def remote(src, dst, ssem, rsem, device):
        return pltpu.make_async_remote_copy(
            src_ref=src, dst_ref=dst, send_sem=ssem, recv_sem=rsem, device_id=device, device_id_type=MESH
        )

    xload = pltpu.make_async_copy(hidden.reshape(TOKENS, hidden.shape[2]), xn, local_sem.at[0])
    kload = pltpu.make_async_copy(kcache, kc, local_sem.at[1])
    vload = pltpu.make_async_copy(vcache, vc, local_sem.at[2])
    xload.start()

    def slot(j, zz, ll, cc):
        return wbuf.at[j, pl.ds(al(((zz * 2 + ll) * 2 + cc) * BLOCK, BLOCK), BLOCK)]

    place = (
        (z, lo), (zp, lo), (zm, lo), (z, 1 - lo), (zp, 1 - lo), (zm, 1 - lo), ((z + 2) % 4, lo), ((z + 2) % 4, 1 - lo)
    )

    def held(j, kind, cc=c):
        return slot(j, place[kind][0], place[kind][1], cc)

    def gput(j, index, src, dst, kind, device):
        remote(src, dst, gsend.at[j, index], grecv.at[j, kind], device).start()

    def gput_same(j, index, ref, kind, device):
        gput(j, index, ref, ref, kind, device)

    def gwait(j, kind):
        ref = held(j, kind % 8, c if kind < 8 else 1 - c)
        remote(ref, ref, gsend.at[j, 0], grecv.at[j, kind], d_sib).wait_recv()

    def first_a(j):
        def proj(source, width, head):
            def cols(tt):
                return source.at[:, pl.ds(al(tt * width + head * LANES, LANES), LANES)]

            pltpu.make_async_copy(cols(t), held(j, 0), grecv.at[j, 0]).start()
            gput(j, 2, cols(y * 2 + 1 - hi), held(j, 0), 3, d_cross)

        @pl.when(j == 0)
        def _():
            proj(wk, LANES, 0)

        @pl.when(j == 1)
        def _():
            proj(wv, LANES, 0)

        @pl.when(jnp.logical_and(j >= 2, j < PROJ_JOBS))
        def _():
            proj(wq, GROUP * LANES, j - 2)

        @pl.when(j >= PROJ_JOBS)
        def _():
            def rows(half):
                return wo.at[
                    pl.ds(al(half * 2048 + (j - PROJ_JOBS) * BLOCK, BLOCK), BLOCK), pl.ds(al(y * LANES, LANES), LANES)
                ]

            @pl.when(c_is_hi)
            def _():
                pltpu.make_async_copy(rows(c), held(j, 0), grecv.at[j, 0]).start()
                pltpu.make_async_copy(rows(1 - c), held(j, 0, 1 - c), grecv.at[j, 8]).start()
                gput(j, 2, rows(1 - c), held(j, 0, 1 - c), 0, d_sib)
                gput(j, 7, rows(c), held(j, 0), 8, d_sib)

            @pl.when(jnp.logical_not(c_is_hi))
            def _():
                gput(j, 2, rows(c), held(j, 0), 3, d_cross)
                gput(j, 7, rows(1 - c), held(j, 0, 1 - c), 3, d_cross_sib)

    def first_b(j):
        gwait(j, 0)
        own = held(j, 0)
        gput_same(j, 0, own, 2, d_zp)
        gput_same(j, 1, own, 1, d_zm)

        @pl.when(j < PROJ_JOBS)
        def _():
            gput_same(j, 7, own, 8, d_sib)

    def to_sib(j, kind):
        gput_same(j, 7 + kind, held(j, kind), 8 + kind, d_sib)

    def mid1(j):
        even = j % 2 == 0
        gwait(j, 1)
        gput_same(j, 3, held(j, 1), 4, d_pair)

        @pl.when(even)
        def _():
            gput_same(j, 5, held(j, 1), 6, d_zm)

        to_sib(j, 1)
        gwait(j, 2)
        gput_same(j, 4, held(j, 2), 5, d_pair)

        @pl.when(jnp.logical_not(even))
        def _():
            gput_same(j, 5, held(j, 2), 6, d_zp)

        to_sib(j, 2)
        gwait(j, 3)
        to_sib(j, 3)

    def mid2(j):
        even = j % 2 == 0
        gwait(j, 4)

        @pl.when(even)
        def _():
            gput_same(j, 6, held(j, 4), 7, d_zm)

        to_sib(j, 4)
        gwait(j, 5)

        @pl.when(jnp.logical_not(even))
        def _():
            gput_same(j, 6, held(j, 5), 7, d_zp)

        to_sib(j, 5)
        gwait(j, 6)
        to_sib(j, 6)

    def fin(j):
        gwait(j, 7)
        to_sib(j, 7)
        for kind in range(8, 16):
            gwait(j, kind)

    def gdone(j):
        for index in range(SENDS):
            ref = held(j, 0)
            remote(ref, ref, gsend.at[j, index], grecv.at[j, 0], d_sib).wait_send()

    y2 = (y + 2) % 4
    peer = ((y, hi), (yp, hi), (ym, hi), (y, 1 - hi), (yp, 1 - hi), (ym, 1 - hi), (y2, hi), (y2, 1 - hi))

    class Ring:
        def __init__(self, ssem, rsem, ref_of):
            self.ssem, self.rsem, self.ref_of = ssem, rsem, ref_of

        def at(self, j, kind):
            return self.ref_of(j, peer[kind][0], peer[kind][1])

        def put(self, j, index, src, kind_here, kind, device):
            remote(src, self.at(j, kind_here), self.ssem.at[j, index], self.rsem.at[j, kind], device).start()

        def forward(self, j, index, kind_here, kind, device):
            self.put(j, index, self.at(j, kind_here), kind_here, kind, device)

        def wait(self, j, kind):
            ref = self.at(j, kind)
            remote(ref, ref, self.ssem.at[j, 0], self.rsem.at[j, kind], d_sib).wait_recv()

        def begin(self, j, src):
            self.put(j, 0, src, 0, 2, d_yp)
            self.put(j, 1, src, 0, 1, d_ym)
            self.put(j, 2, src, 0, 3, d_hi)

        def mid1(self, j):
            even = j % 2 == 0
            self.wait(j, 1)

            @pl.when(even)
            def _():
                self.forward(j, 3, 1, 6, d_ym)

            self.wait(j, 2)

            @pl.when(jnp.logical_not(even))
            def _():
                self.forward(j, 3, 2, 6, d_yp)

            self.wait(j, 3)
            self.forward(j, 4, 3, 5, d_yp)
            self.forward(j, 5, 3, 4, d_ym)

        def mid2(self, j):
            self.wait(j, 6)
            self.forward(j, 6, 6, 7, d_hi)
            self.wait(j, 4)
            self.wait(j, 5)

        def fin(self, j):
            self.wait(j, 7)

        def done(self, j):
            ref = self.at(j, 0)
            for index in range(7):
                remote(ref, ref, self.ssem.at[j, index], self.rsem.at[j, 1], d_sib).wait_send()

    out2 = out.reshape(TOKENS, out.shape[2])

    def ctx_block(j, yy, hh):
        return ctx.at[yy * 2 + hh, pl.ds(al(j * CHUNK, CHUNK), CHUNK)]

    def out_block(j, yy, hh):
        return out2.at[:, pl.ds(al((j * 2 + hh) * 512 + yy * LANES, LANES), LANES)]

    ctx_ring = Ring(csend, crecv, ctx_block)
    out_ring = Ring(osend, orecv, out_block)

    def norm(i):
        rows = pl.ds(al(i * 64, 64), 64)
        width = xn.shape[1]

        def square(k, total):
            v = xn[rows, pl.ds(al(k * 512, 512), 512)].astype(f32)
            v = v * v
            return total + (v[:, :128] + v[:, 128:256]) + (v[:, 256:384] + v[:, 384:])

        total = lax.fori_loop(0, width // 512, square, jnp.zeros((64, 128), f32))
        scale = lax.rsqrt(jnp.sum(total, axis=1, keepdims=True) * (1.0 / width) + epsilon)

        def apply(k, _):
            cols = pl.ds(al(k * 512, 512), 512)
            xn[rows, cols] = (xn[rows, cols].astype(f32) * scale).astype(bf16)
            return 0

        lax.fori_loop(0, width // 512, apply, 0)

    def project(j):
        acc[...] = jnp.zeros_like(acc)

        def part(k, _):
            cols = pl.ds(al(k * 1024, 1024), 1024)
            acc[...] += jnp.dot(xn[:, cols], wbuf[j, cols, :], preferred_element_type=f32)
            return 0

        lax.fori_loop(0, 8, part, 0)

        @pl.when(j == 1)
        def _():
            vn[...] = acc[...].astype(bf16)

        @pl.when(j != 1)
        def _():
            v = acc[...]
            rotated = (v * cos_ref[...] + pltpu.roll(v, HD // 2, 1) * sin_ref[...]).astype(bf16)

            @pl.when(j == 0)
            def _():
                kn[...] = rotated

            @pl.when(j >= 2)
            def _():
                qr[j - 2] = rotated

    scaling = 1.0 / math.sqrt(HD)
    nt = (((1,), (1,)), ((), ()))

    def attend(i):
        def block(b, _):
            tok = al(i * CHUNK + b * 16, 16)
            q = jnp.concatenate([qr[g, pl.ds(tok, 16), :] for g in range(GROUP)], axis=0)
            slots = pl.ds(al((i * 32 + b * 4) * 128, 512), 512)
            fresh = pl.ds(al(i * CHUNK, CHUNK), CHUNK)
            older = lax.dot_general(q, kc[slots, :], nt, preferred_element_type=f32) * scaling
            recent = lax.dot_general(q, kn[fresh, :], nt, preferred_element_type=f32) * scaling
            live = len_ref[pl.ds(tok, 16), :1]
            live = jnp.concatenate([live] * GROUP, axis=0)
            token = lax.broadcasted_iota(jnp.int32, (16 * GROUP, 1), 0) % 16
            row = token // STEPS
            lane = lax.broadcasted_iota(jnp.int32, older.shape, 1)
            older = jnp.where((lane >= row * 128) & (lane < row * 128 + live), older, masked)
            lane = lax.broadcasted_iota(jnp.int32, recent.shape, 1) - b * 16
            recent = jnp.where((lane >= row * STEPS) & (lane <= token), recent, masked)
            highest = jnp.maximum(jnp.max(older, axis=1, keepdims=True), jnp.max(recent, axis=1, keepdims=True))
            older = jnp.exp(older - highest)
            recent = jnp.exp(recent - highest)
            total = jnp.sum(older, axis=1, keepdims=True) + jnp.sum(recent, axis=1, keepdims=True)
            inverse = 1.0 / total
            mix = jnp.dot((older * inverse).astype(bf16), vc[slots, :], preferred_element_type=f32)
            mix += jnp.dot((recent * inverse).astype(bf16), vn[fresh, :], preferred_element_type=f32)
            mix = mix.astype(bf16)
            for g in range(GROUP):
                ctx[t, pl.ds(tok, 16), g * HD:(g + 1) * HD] = mix[g * 16:(g + 1) * 16]
            return 0

        lax.fori_loop(0, 8, block, 0)

    def out_unit(u):
        acc[...] = jnp.zeros_like(acc)

        def part(tt, _):
            weights = wbuf[PROJ_JOBS + tt % 4, pl.ds(al((u * 2 + tt // 4) * BLOCK, BLOCK), BLOCK), :]
            acc[...] += jnp.dot(ctx[tt], weights, preferred_element_type=f32)
            return 0

        lax.fori_loop(0, TP, part, 0)
        obuf[u] = acc[...].astype(bf16)

    barrier = pltpu.get_barrier_semaphore()
    partners = (d_zp, d_zm, d_yp, d_ym, d_pair, d_hi, d_sib, d_cross, d_cross_sib)
    for device in partners:
        pl.semaphore_signal(barrier, inc=1, device_id=device, device_id_type=MESH)
    pl.semaphore_wait(barrier, len(partners))

    first_a(jnp.int32(0))
    first_a(jnp.int32(1))
    kload.start()
    vload.start()
    first_b(jnp.int32(0))
    xload.wait()

    def within(j, low, high, run):
        @pl.when(jnp.logical_and(j >= low, j < high))
        def _():
            run(j)

    steps = JOBS + 2

    def step(s, _):
        within(s + 2, 0, JOBS, first_a)
        within(s + 1, 0, JOBS, first_b)

        @pl.when(s < 2)
        def _():
            def some(i, _):
                norm(s * 4 + i)
                return 0

            lax.fori_loop(0, 4, some, 0)

        within(s, 0, JOBS, mid1)
        within(s - 1, 0, JOBS, mid2)
        within(s - 2, 0, JOBS, fin)
        within(s - 2, 0, PROJ_JOBS, project)

        @pl.when(s == PROJ_JOBS + 2)
        def _():
            kload.wait()
            vload.wait()

        @pl.when(jnp.logical_and(s >= PROJ_JOBS + 2, s < PROJ_JOBS + 2 + CHUNKS))
        def _():
            i = s - (PROJ_JOBS + 2)
            attend(i)
            ctx_ring.begin(i, ctx_block(i, y, hi))

        within(s - (PROJ_JOBS + 3), 0, CHUNKS, ctx_ring.mid1)
        within(s - (PROJ_JOBS + 4), 0, CHUNKS, ctx_ring.mid2)
        within(s - (PROJ_JOBS + 5), 0, CHUNKS, ctx_ring.fin)
        within(s - 4, 0, JOBS, gdone)
        return 0

    lax.fori_loop(0, steps, step, 0)
    ctx_ring.mid1(CHUNKS - 1)
    ctx_ring.mid2(CHUNKS - 2)
    ctx_ring.fin(CHUNKS - 3)
    ctx_ring.mid2(CHUNKS - 1)
    ctx_ring.fin(CHUNKS - 2)
    ctx_ring.fin(CHUNKS - 1)

    def ostep(u, _):
        @pl.when(u < UNITS)
        def _():
            out_unit(u)
            pltpu.make_async_copy(obuf.at[u], out_ring.at(u, 0), local_sem.at[3 + u]).start()
            out_ring.begin(u, obuf.at[u])

        within(u - 1, 0, UNITS, out_ring.mid1)
        within(u - 2, 0, UNITS, out_ring.mid2)
        within(u - 3, 0, UNITS, out_ring.fin)
        within(u - 3, 0, UNITS, out_ring.done)
        return 0

    lax.fori_loop(0, UNITS + 3, ostep, 0)
    for u in range(UNITS):
        pltpu.make_async_copy(obuf.at[u], out_ring.at(u, 0), local_sem.at[3 + u]).wait()
    for j in range(steps - 4, JOBS):
        gdone(j)
    for j in range(CHUNKS):
        ctx_ring.done(j)


def body(
    hidden_in, lengths, key_cache, value_cache, query_weight, key_weight, value_weight, out_weight
):
    row_count, step_count, width = hidden_in.shape
    slots = key_cache.shape[1]
    offsets = lax.broadcasted_iota(jnp.int32, (row_count, step_count), 1)
    positions = (lengths[:, None] + offsets).reshape(TOKENS)
    frequency = rope_base ** (-(jnp.arange(HD // 2, dtype=f32) * 2.0) / HD)
    angles = positions.astype(f32)[:, None] * frequency
    cosine, sine = jnp.cos(angles), jnp.sin(angles)
    cosine = jnp.concatenate([cosine, cosine], axis=1)
    sine = jnp.concatenate([-sine, sine], axis=1)
    live = jnp.broadcast_to(jnp.repeat(lengths, step_count)[:, None], (TOKENS, LANES))
    hbm = pl.BlockSpec(memory_space=pl.ANY)
    vmem = pl.BlockSpec(memory_space=pltpu.VMEM)
    dma = pltpu.SemaphoreType.DMA
    return pl.pallas_call(
        layer_kernel,
        out_shape=jax.ShapeDtypeStruct(hidden_in.shape, bf16),
        in_specs=[hbm] * 7 + [vmem] * 3,
        out_specs=hbm,
        scratch_shapes=[
            pltpu.VMEM((JOBS, width, LANES), bf16),
            pltpu.VMEM((TOKENS, width), bf16),
            pltpu.VMEM((row_count * slots, HD), bf16),
            pltpu.VMEM((row_count * slots, HD), bf16),
            pltpu.VMEM((GROUP, TOKENS, HD), bf16),
            pltpu.VMEM((TOKENS, HD), bf16),
            pltpu.VMEM((TOKENS, HD), bf16),
            pltpu.VMEM((TP, TOKENS, GROUP * HD), bf16),
            pltpu.VMEM((UNITS, TOKENS, LANES), bf16),
            pltpu.VMEM((TOKENS, LANES), f32),
            dma((JOBS, SENDS)),
            dma((JOBS, 16)),
            dma((CHUNKS, 7)),
            dma((CHUNKS, 8)),
            dma((UNITS, 7)),
            dma((UNITS, 8)),
            dma((3 + UNITS,)),
        ],
        compiler_params=pltpu.CompilerParams(
            collective_id=0, has_side_effects=True, vmem_limit_bytes=60 * 1024 * 1024
        ),
        name="attention_layer",
    )(
        hidden_in,
        key_cache.reshape(row_count * slots, HD),
        value_cache.reshape(row_count * slots, HD),
        query_weight, key_weight, value_weight, out_weight, cosine, sine, live,
    )


def solution(mesh):
    return jax.shard_map(
        body,
        mesh=mesh,
        in_specs=(
            P("fsdp", None, None),
            P("fsdp"),
            P("fsdp", None, "tp"),
            P("fsdp", None, "tp"),
            P("fsdp", None),
            P("fsdp", None),
            P("fsdp", None),
            P(None, "fsdp"),
        ),
        out_specs=P("fsdp", None, None),
        check_vma=False,
    )
```

```python
import math

import jax
import jax.numpy as jnp
import numpy as np
from jax import lax
from jax.experimental import pallas as pl
from jax.experimental.pallas import tpu as pltpu
from jax.sharding import PartitionSpec as P

HD = 128
STEPS = 4
GROUP = 4
LANES = 128
rope_base = 1000000.0
epsilon = 1e-06
masked = -1e30

MESH = pl.DeviceIdType.MESH
f32 = jnp.float32
bf16 = jnp.bfloat16

JOBS = 6
QUARTERS = 4
BLOCK = 512
TOKENS = 512
HALF = TOKENS // 2
TP = 8
UNITS = (0, 3, 1, 2, 4, 5, 6, 7)


def al(x, m):
    return pl.multiple_of(x, m)


def layer_kernel(
    hidden, kcache, vcache, wq, wk, wv, wo, lengths, frequency,
    out,
    wbuf, wobuf, xn, kc, vc, qr, kn, vn, ctx, acc, cos_ref, sin_ref, len_ref,
    gsend, grecv, gsib, wsend, wrecv, wsib, csend, crecv, osend, orecv, local_sem,
):
    f, t = lax.axis_index("fsdp"), lax.axis_index("tp")
    z, lo, c = f // 4, (f // 2) % 2, f % 2
    y, hi = t // 2, t % 2
    c_is_hi = c == hi

    def dev(zz=z, ll=lo, cc=c, yy=y, hh=hi):
        return (zz * 4 + ll * 2 + cc, yy * 2 + hh)

    zp, zm, z2 = (z + 1) % 4, (z + 3) % 4, (z + 2) % 4
    yp, ym, y2 = (y + 1) % 4, (y + 3) % 4, (y + 2) % 4
    d_zp, d_zm = dev(zz=zp), dev(zz=zm)
    d_yp, d_ym = dev(yy=yp), dev(yy=ym)
    d_pair, d_hi, d_sib = dev(ll=1 - lo), dev(hh=1 - hi), dev(cc=1 - c)
    d_cross = dev(ll=1 - lo, hh=1 - hi)
    d_cross_sib = dev(ll=1 - lo, hh=1 - hi, cc=1 - c)

    def remote(src, dst, ssem, rsem, device):
        return pltpu.make_async_remote_copy(
            src_ref=src, dst_ref=dst, send_sem=ssem, recv_sem=rsem, device_id=device, device_id_type=MESH
        )

    place = ((z, lo), (zp, lo), (zm, lo), (z, 1 - lo), (zp, 1 - lo), (zm, 1 - lo), (z2, lo), (z2, 1 - lo))

    def group(kind):
        return (0, 1, 1, 0, 2, 2, 3, 3)[kind]

    class Gather:
        def __init__(self, buffer, ssem, rsem, sib_sem):
            self.buffer, self.ssem, self.rsem, self.sib_sem = buffer, ssem, rsem, sib_sem

        def held(self, j, kind, cc=c):
            zz, ll = place[kind]
            return self.buffer.at[j, pl.ds(al(((zz * 2 + ll) * 2 + cc) * BLOCK, BLOCK), BLOCK)]

        def load(self, j, src, kind):
            if kind < 8:
                pltpu.make_async_copy(src, self.held(j, kind), self.rsem.at[j, kind]).start()
            else:
                pltpu.make_async_copy(src, self.held(j, kind - 8, 1 - c), self.sib_sem(j, kind - 8)).start()

        def put(self, j, src, dst, kind, device):
            sem = self.rsem.at[j, kind] if kind < 8 else self.sib_sem(j, kind - 8)
            remote(src, dst, self.ssem.at[j], sem, device).start()

        def pass_on(self, j, kind_here, kind, device):
            ref = self.held(j, kind_here)
            self.put(j, ref, ref, kind, device)

        def to_sib(self, j, kind):
            self.pass_on(j, kind, 8 + kind, d_sib)

        def wait(self, j, kind):
            ref = self.held(j, kind)
            remote(ref, ref, self.ssem.at[j], self.rsem.at[j, kind], d_sib).wait_recv()

        def wait_sib(self, sem):
            ref = self.buffer.at[0, pl.ds(0, 8 * BLOCK)]
            remote(ref, ref, self.ssem.at[0], sem, d_sib).wait_recv()

        def sent(self, j, count):
            ref = self.buffer.at[j, pl.ds(0, count * BLOCK)]
            remote(ref, ref, self.ssem.at[j], self.rsem.at[j, 0], d_sib).wait_send()

    proj = Gather(wbuf, gsend, grecv, lambda j, kind: gsib.at[j])
    outw = Gather(wobuf, wsend, wrecv, lambda q, kind: wsib.at[group(kind)])

    def source_of(j):
        return ((wk, LANES, 0), (wv, LANES, 0))[j] if j < 2 else (wq, GROUP * LANES, j - 2)

    def first_a(j):
        source, width, head = source_of(j)
        proj.load(j, source.at[:, pl.ds(al(t * width + head * LANES, LANES), LANES)], 0)

    def first_x(j):
        source, width, head = source_of(j)
        cols = source.at[:, pl.ds(al((y * 2 + 1 - hi) * width + head * LANES, LANES), LANES)]
        proj.put(j, cols, proj.held(j, 0), 3, d_cross)

    def first_b(j):
        proj.wait(j, 0)
        proj.pass_on(j, 0, 2, d_zp)
        proj.pass_on(j, 0, 1, d_zm)
        proj.to_sib(j, 0)

    def mid1(j):
        proj.wait(j, 1)
        proj.pass_on(j, 1, 4, d_pair)
        proj.wait(j, 2)
        proj.pass_on(j, 2, 5, d_pair)
        if j % 2 == 0:
            proj.pass_on(j, 1, 6, d_zm)
        else:
            proj.pass_on(j, 2, 6, d_zp)
        proj.to_sib(j, 1)
        proj.to_sib(j, 2)
        proj.wait(j, 3)
        proj.to_sib(j, 3)

    def mid2(j):
        proj.wait(j, 4)
        if j % 2 == 0:
            proj.pass_on(j, 4, 7, d_zm)
        proj.to_sib(j, 4)
        proj.wait(j, 5)
        if j % 2 == 1:
            proj.pass_on(j, 5, 7, d_zp)
        proj.to_sib(j, 5)
        proj.wait(j, 6)
        proj.to_sib(j, 6)

    def fin(j):
        proj.wait(j, 7)
        proj.to_sib(j, 7)
        proj.wait_sib(gsib.at[j])

    def ow_rows(q, half):
        return wo.at[pl.ds(al(half * 2048 + q * BLOCK, BLOCK), BLOCK), pl.ds(al(y * LANES, LANES), LANES)]

    def ow_load():
        for q in range(QUARTERS):
            @pl.when(c_is_hi)
            def _():
                outw.load(q, ow_rows(q, c), 0)
                outw.load(q, ow_rows(q, 1 - c), 8)
                outw.put(q, ow_rows(q, 1 - c), outw.held(q, 0, 1 - c), 0, d_sib)
                outw.put(q, ow_rows(q, c), outw.held(q, 0), 8, d_sib)

    def ow_first():
        for q in range(QUARTERS):
            outw.wait(q, 0)
            outw.pass_on(q, 0, 2, d_zp)
            outw.pass_on(q, 0, 1, d_zm)
            if q % 2 == 0:
                outw.pass_on(q, 0, 3, d_pair)
            else:
                @pl.when(jnp.logical_not(c_is_hi))
                def _():
                    outw.put(q, ow_rows(q, c), outw.held(q, 0), 3, d_cross)
                    outw.put(q, ow_rows(q, 1 - c), outw.held(q, 0, 1 - c), 3, d_cross_sib)

    def ow_second():
        for q in range(QUARTERS):
            outw.wait(q, 3)
            outw.pass_on(q, 3, 5, d_zp)
            outw.pass_on(q, 3, 4, d_zm)
            outw.to_sib(q, 3)
        for q in range(QUARTERS):
            for kind in (1, 2):
                outw.wait(q, kind)
                outw.to_sib(q, kind)
            if q % 2 == 0:
                outw.pass_on(q, 1, 6, d_zm)
            else:
                outw.pass_on(q, 2, 6, d_zp)

    def ow_third():
        for q in range(QUARTERS):
            for kind in (4, 5):
                outw.wait(q, kind)
                outw.to_sib(q, kind)
            if q % 2 == 0:
                outw.pass_on(q, 4, 7, d_zm)
            else:
                outw.pass_on(q, 5, 7, d_zp)

    def ow_last():
        for q in range(QUARTERS):
            for kind in (6, 7):
                outw.wait(q, kind)
                outw.to_sib(q, kind)

    def ow_ready(i):
        outw.wait_sib(wsib.at[i])

    peer = ((y, hi), (yp, hi), (ym, hi), (y, 1 - hi), (yp, 1 - hi), (ym, 1 - hi), (y2, hi), (y2, 1 - hi))

    class Ring:
        def __init__(self, ssem, rsem, block, seven):
            self.ssem, self.rsem, self.block, self.seven = ssem, rsem, block, seven

        def at(self, j, kind):
            return self.block(j, peer[kind][0], peer[kind][1])

        def forward(self, j, kind_here, kind, device):
            ref = self.at(j, kind_here)
            remote(ref, ref, self.ssem.at[j], self.rsem.at[j, kind], device).start()

        def wait(self, j, kind):
            ref = self.at(j, kind)
            remote(ref, ref, self.ssem.at[j], self.rsem.at[j, kind], d_sib).wait_recv()

        def begin(self, j):
            self.forward(j, 0, 2, d_yp)
            self.forward(j, 0, 1, d_ym)
            self.forward(j, 0, 3, d_hi)

        def mid1(self, j):
            self.wait(j, 1)
            if j % 2 == 0:
                self.forward(j, 1, 6, d_ym)
            self.wait(j, 2)
            if j % 2 == 1:
                self.forward(j, 2, 6, d_yp)
            self.wait(j, 3)
            self.forward(j, 3, 5, d_yp)
            self.forward(j, 3, 4, d_ym)

        def mid2(self, j):
            self.wait(j, 6)
            self.forward(j, 6, 7, d_hi)
            self.wait(j, 4)
            self.wait(j, 5)

        def fin(self, j):
            self.wait(j, 7)

        def done(self, j):
            remote(self.seven, self.seven, self.ssem.at[j], self.rsem.at[j, 1], d_sib).wait_send()

    def ctx_block(j, yy, hh):
        return ctx.at[yy * 2 + hh, j // 2, pl.ds((j % 2) * HALF, HALF)]

    def out_cols(j, yy, hh):
        zz, ll = place[UNITS[j]]
        return pl.ds(al(((zz * 2 + ll) * 2 + hh) * BLOCK + yy * LANES, LANES), LANES)

    def out_block(j, yy, hh):
        return out.at[:, out_cols(j, yy, hh)]

    ctx_ring = Ring(csend, crecv, ctx_block, ctx.at[pl.ds(0, 7), 0, pl.ds(0, HALF)])
    out_ring = Ring(osend, orecv, out_block, out.at[:, pl.ds(0, 7 * LANES)])

    def tables():
        def part(i, _):
            rows = pl.ds(al(i * 64, 64), 64)
            token = lax.broadcasted_iota(jnp.int32, (64, LANES), 0) + i * 64
            lane = lax.broadcasted_iota(jnp.int32, (64, LANES), 1)
            mine = jnp.where(lane == token // STEPS, lengths[...].astype(f32), 0.0)
            live = jnp.sum(mine, axis=1, keepdims=True)
            len_ref[rows, :] = jnp.broadcast_to(live, (64, LANES)).astype(jnp.int32)
            angles = (live + (token % STEPS).astype(f32)) * frequency[...]
            cos_ref[rows, :] = jnp.cos(angles)
            sine = jnp.sin(angles)
            sin_ref[rows, :] = jnp.where(lane < HD // 2, -sine, sine)
            return 0

        lax.fori_loop(0, TOKENS // 64, part, 0)

    def norm(i, _):
        rows = pl.ds(al(i * 64, 64), 64)
        width = xn.shape[1]

        def square(k, total):
            v = xn[rows, pl.ds(al(k * 512, 512), 512)].astype(f32)
            v = v * v
            return total + (v[:, :128] + v[:, 128:256]) + (v[:, 256:384] + v[:, 384:])

        total = lax.fori_loop(0, width // 512, square, jnp.zeros((64, 128), f32))
        scale = lax.rsqrt(jnp.sum(total, axis=1, keepdims=True) * (1.0 / width) + epsilon)

        def apply(k, _):
            cols = pl.ds(al(k * 512, 512), 512)
            xn[rows, cols] = (xn[rows, cols].astype(f32) * scale).astype(bf16)
            return 0

        lax.fori_loop(0, width // 512, apply, 0)
        return 0

    def project(p):
        acc[...] = jnp.zeros_like(acc)

        def part(k, _):
            cols = pl.ds(al(k * 1024, 1024), 1024)
            weights = jnp.concatenate([wbuf[2 * p, cols, :], wbuf[2 * p + 1, cols, :]], axis=1)
            acc[...] += jnp.dot(xn[:, cols], weights, preferred_element_type=f32)
            return 0

        lax.fori_loop(0, 8, part, 0)

        def rotated(v):
            return (v * cos_ref[...] + pltpu.roll(v, HD // 2, 1) * sin_ref[...]).astype(bf16)

        if p == 0:
            kn[...] = rotated(acc[:, :HD])
            vn[...] = acc[:, HD:].astype(bf16)
        else:
            qr[2 * p - 2] = rotated(acc[:, :HD])
            qr[2 * p - 1] = rotated(acc[:, HD:])

    scaling = 1.0 / math.sqrt(HD)
    nt = (((1,), (1,)), ((), ()))

    def attend(p, i):
        fresh = slice(i * 128, (i + 1) * 128)
        token = lax.broadcasted_iota(jnp.int32, (32, 1), 0) % 16
        row = token // STEPS
        scores = []
        for b in range(8):
            tok = slice(i * 128 + b * 16, i * 128 + (b + 1) * 16)
            q = jnp.concatenate([qr[2 * p, tok, :], qr[2 * p + 1, tok, :]], axis=0)
            keys = kc[(i * 8 + b) * 512:(i * 8 + b + 1) * 512, :]
            older = lax.dot_general(q, keys, nt, preferred_element_type=f32) * scaling
            recent = lax.dot_general(q, kn[fresh, :], nt, preferred_element_type=f32) * scaling
            scores.append((older, recent))
        for b in range(8):
            older, recent = scores[b]
            live = len_ref[i * 128 + b * 16:i * 128 + (b + 1) * 16, :1]
            live = jnp.concatenate([live, live], axis=0)
            lane = lax.broadcasted_iota(jnp.int32, older.shape, 1)
            older = jnp.where((lane >= row * 128) & (lane < row * 128 + live), older, masked)
            lane = lax.broadcasted_iota(jnp.int32, recent.shape, 1) - b * 16
            recent = jnp.where((lane >= row * STEPS) & (lane <= token), recent, masked)
            scores[b] = older, recent
        highest = [
            jnp.maximum(jnp.max(older, axis=1, keepdims=True), jnp.max(recent, axis=1, keepdims=True))
            for older, recent in scores
        ]
        scores = [(jnp.exp(older - h), jnp.exp(recent - h)) for (older, recent), h in zip(scores, highest)]
        inverse = [
            1.0 / (jnp.sum(older, axis=1, keepdims=True) + jnp.sum(recent, axis=1, keepdims=True))
            for older, recent in scores
        ]
        mixes = []
        for b in range(8):
            older, recent = scores[b]
            values = vc[(i * 8 + b) * 512:(i * 8 + b + 1) * 512, :]
            mix = jnp.dot((older * inverse[b]).astype(bf16), values, preferred_element_type=f32)
            mix += jnp.dot((recent * inverse[b]).astype(bf16), vn[fresh, :], preferred_element_type=f32)
            mixes.append(mix.astype(bf16))
        for b in range(8):
            tok = slice(i * 128 + b * 16, i * 128 + (b + 1) * 16)
            ctx[t, p, tok, :] = jnp.concatenate([mixes[b][:16], mixes[b][16:]], axis=1)

    def out_units(j):
        acc[...] = jnp.zeros_like(acc)
        slots = [(place[UNITS[j + i]][0] * 2 + place[UNITS[j + i]][1]) * 2 for i in range(2)]

        def part(i, _):
            def weights(tt):
                half = tt // 4
                pieces = [wobuf[tt % 4, pl.ds(al((slot + half) * BLOCK, BLOCK), BLOCK), :] for slot in slots]
                return jnp.concatenate(pieces, axis=1)

            left = jnp.concatenate([ctx[2 * i, 0], ctx[2 * i, 1], ctx[2 * i + 1, 0], ctx[2 * i + 1, 1]], axis=1)
            right = jnp.concatenate([weights(2 * i), weights(2 * i + 1)], axis=0)
            acc[...] += jnp.dot(left, right, preferred_element_type=f32)
            return 0

        lax.fori_loop(0, TP // 2, part, 0)
        for i in range(2):
            out[:, out_cols(j + i, y, hi)] = acc[:, i * LANES:(i + 1) * LANES].astype(bf16)

    xload = pltpu.make_async_copy(hidden.reshape(TOKENS, hidden.shape[2]), xn, local_sem.at[0])
    kload = pltpu.make_async_copy(kcache, kc, local_sem.at[1])
    vload = pltpu.make_async_copy(vcache, vc, local_sem.at[2])
    barrier = pltpu.get_barrier_semaphore()
    partners = (d_hi, d_zp, d_zm, d_yp, d_ym, d_pair, d_cross, d_cross_sib, d_sib)
    for device in partners:
        pl.semaphore_signal(barrier, inc=1, device_id=device, device_id_type=MESH)
    for j in range(3):
        first_a(j)
    xload.start()
    kload.start()
    vload.start()
    tables()
    pl.semaphore_wait(barrier, len(partners))
    for j in range(2):
        first_x(j)
        first_b(j)
    xload.wait()
    lax.fori_loop(0, TOKENS // 64, norm, 0)
    for j in range(4):
        mid1(j)
        first_x(j + 2)
        first_b(j + 2)
        if j < 3:
            first_a(j + 3)
        if j >= 1:
            mid2(j - 1)
        if j >= 2:
            fin(j - 2)
    project(0)
    mid1(4)
    mid2(3)
    fin(2)
    ow_load()
    mid1(5)
    mid2(4)
    fin(3)
    project(1)
    kload.wait()
    vload.wait()
    mid2(5)
    ow_first()
    attend(0, 0)
    attend(0, 1)
    ctx_ring.begin(0)
    fin(4)
    attend(0, 2)
    attend(0, 3)
    ctx_ring.begin(1)
    fin(5)
    project(2)
    ctx_ring.mid1(0)
    attend(1, 0)
    attend(1, 1)
    ctx_ring.begin(2)
    ctx_ring.mid1(1)
    attend(1, 2)
    attend(1, 3)
    ctx_ring.begin(3)
    ow_second()
    ctx_ring.mid2(0)
    ctx_ring.mid1(2)
    ctx_ring.mid2(1)
    ctx_ring.mid1(3)
    ow_third()
    ctx_ring.mid2(2)
    ctx_ring.mid2(3)
    for j in range(4):
        ctx_ring.fin(j)
    for j in range(8):
        if j == 2:
            ow_last()
        if j % 2 == 0:
            ow_ready(j // 2)
            out_units(j)
        out_ring.begin(j)
        if j >= 1:
            out_ring.mid1(j - 1)
        if j >= 2:
            out_ring.mid2(j - 2)
    for j in range(JOBS):
        proj.sent(j, 15)
    out_ring.mid1(7)
    out_ring.mid2(6)
    for q in range(QUARTERS):
        if q % 2 == 1:
            outw.sent(q, 15)
        else:
            @pl.when(c_is_hi)
            def _():
                outw.sent(q, 16)

            @pl.when(jnp.logical_not(c_is_hi))
            def _():
                outw.sent(q, 14)
    for j in range(4):
        ctx_ring.done(j)
    out_ring.mid2(7)
    for j in range(8):
        out_ring.fin(j)
    for j in range(8):
        out_ring.done(j)


def place_result(held, out, sem):
    flat = out.reshape(held.shape)
    copies = []
    for i in range(4):
        rows = pl.ds(i * 128, 128)
        copies.append(pltpu.make_async_copy(held.at[rows], flat.at[rows], sem.at[i]))
        copies[-1].start()
    for copy in copies:
        copy.wait()


def body(
    hidden_in, lengths, key_cache, value_cache, query_weight, key_weight, value_weight, out_weight
):
    row_count, step_count, width = hidden_in.shape
    slots = key_cache.shape[1]
    frequency = np.tile(rope_base ** (-(np.arange(HD // 2) * 2.0) / HD), 2).astype(np.float32)[None, :]
    hbm = pl.BlockSpec(memory_space=pl.ANY)
    vmem = pl.BlockSpec(memory_space=pltpu.VMEM)
    dma = pltpu.SemaphoreType.DMA
    result = pl.pallas_call(
        layer_kernel,
        out_shape=pltpu.VMEM((TOKENS, width), bf16),
        in_specs=[hbm] * 7 + [vmem] * 2,
        out_specs=vmem,
        scratch_shapes=[
            pltpu.VMEM((JOBS, width, LANES), bf16),
            pltpu.VMEM((QUARTERS, width, LANES), bf16),
            pltpu.VMEM((TOKENS, width), bf16),
            pltpu.VMEM((row_count * slots, HD), bf16),
            pltpu.VMEM((row_count * slots, HD), bf16),
            pltpu.VMEM((GROUP, TOKENS, HD), bf16),
            pltpu.VMEM((TOKENS, HD), bf16),
            pltpu.VMEM((TOKENS, HD), bf16),
            pltpu.VMEM((TP, 2, TOKENS, 2 * HD), bf16),
            pltpu.VMEM((TOKENS, 2 * LANES), f32),
            pltpu.VMEM((TOKENS, LANES), f32),
            pltpu.VMEM((TOKENS, LANES), f32),
            pltpu.VMEM((TOKENS, LANES), jnp.int32),
            dma((JOBS,)),
            dma((JOBS, 8)),
            dma((JOBS,)),
            dma((QUARTERS,)),
            dma((QUARTERS, 8)),
            dma((4,)),
            dma((4,)),
            dma((4, 8)),
            dma((8,)),
            dma((8, 8)),
            dma((3,)),
        ],
        compiler_params=pltpu.CompilerParams(
            collective_id=0, has_side_effects=True, vmem_limit_bytes=50 * 1024 * 1024
        ),
        name="attention_layer",
    )(
        hidden_in,
        key_cache.reshape(row_count * slots, HD),
        value_cache.reshape(row_count * slots, HD),
        query_weight, key_weight, value_weight, out_weight,
        lengths.reshape(1, row_count), jnp.asarray(frequency),
    )
    return pl.pallas_call(
        place_result,
        out_shape=jax.ShapeDtypeStruct(hidden_in.shape, bf16),
        in_specs=[vmem],
        out_specs=hbm,
        scratch_shapes=[dma((4,))],
        compiler_params=pltpu.CompilerParams(vmem_limit_bytes=1024 * 1024),
        name="place_result",
    )(result)


def solution(mesh):
    return jax.shard_map(
        body,
        mesh=mesh,
        in_specs=(
            P("fsdp", None, None),
            P("fsdp"),
            P("fsdp", None, "tp"),
            P("fsdp", None, "tp"),
            P("fsdp", None),
            P("fsdp", None),
            P("fsdp", None),
            P(None, "fsdp"),
        ),
        out_specs=P("fsdp", None, None),
        check_vma=False,
    )
```

```python
import math

import jax
import jax.numpy as jnp
import numpy as np
from jax import lax
from jax.experimental import pallas as pl
from jax.experimental.pallas import tpu as pltpu
from jax.sharding import PartitionSpec as P

HD = 128
STEPS = 4
GROUP = 4
LANES = 128
rope_base = 1000000.0
epsilon = 1e-06
masked = -1e30

MESH = pl.DeviceIdType.MESH
f32 = jnp.float32
bf16 = jnp.bfloat16

JOBS = 6
QUARTERS = 4
BLOCK = 512
TOKENS = 512
HALF = TOKENS // 2
TP = 8
UNITS = (0, 3, 1, 2, 4, 5, 6, 7)
OUT_PAIRS = ((0, 0), (0, 2), (1, 0), (1, 2), (0, 4), (1, 4), (0, 6), (1, 6))
OUT_ORDER = tuple((half, u + i) for half, u in OUT_PAIRS for i in range(2))
OUT_JOBS = len(OUT_ORDER)
CTX_ACROSS = (2, 2, 2, 2)
OUT_ACROSS = (2, 2, 3) * 5 + (2,)


def al(x, m):
    return pl.multiple_of(x, m)


def layer_kernel(
    hidden, kcache, vcache, wq, wk, wv, wo, lengths, frequency,
    out,
    wbuf, wobuf, xn, kc, vc, qr, kn, vn, ctx, acc, cos_ref, sin_ref, len_ref,
    gsend, grecv, gsib, wsend, wrecv, wsib, csend, crecv, osend, orecv, local_sem,
):
    f, t = lax.axis_index("fsdp"), lax.axis_index("tp")
    z, lo, c = f // 4, (f // 2) % 2, f % 2
    y, hi = t // 2, t % 2
    c_is_hi = c == hi

    def dev(zz=z, ll=lo, cc=c, yy=y, hh=hi):
        return (zz * 4 + ll * 2 + cc, yy * 2 + hh)

    zp, zm, z2 = (z + 1) % 4, (z + 3) % 4, (z + 2) % 4
    yp, ym, y2 = (y + 1) % 4, (y + 3) % 4, (y + 2) % 4
    d_zp, d_zm = dev(zz=zp), dev(zz=zm)
    d_yp, d_ym = dev(yy=yp), dev(yy=ym)
    d_pair, d_hi, d_sib = dev(ll=1 - lo), dev(hh=1 - hi), dev(cc=1 - c)
    d_cross = dev(ll=1 - lo, hh=1 - hi)
    d_cross_sib = dev(ll=1 - lo, hh=1 - hi, cc=1 - c)

    def remote(src, dst, ssem, rsem, device):
        return pltpu.make_async_remote_copy(
            src_ref=src, dst_ref=dst, send_sem=ssem, recv_sem=rsem, device_id=device, device_id_type=MESH
        )

    place = ((z, lo), (zp, lo), (zm, lo), (z, 1 - lo), (zp, 1 - lo), (zm, 1 - lo), (z2, lo), (z2, 1 - lo))

    def group(kind):
        return (0, 1, 1, 0, 2, 2, 3, 3)[kind]

    class Gather:
        def __init__(self, buffer, ssem, rsem, sib_sem):
            self.buffer, self.ssem, self.rsem, self.sib_sem = buffer, ssem, rsem, sib_sem

        def held(self, j, kind, cc=c):
            zz, ll = place[kind]
            return self.buffer.at[j, pl.ds(al(((zz * 2 + ll) * 2 + cc) * BLOCK, BLOCK), BLOCK)]

        def load(self, j, src, kind):
            if kind < 8:
                pltpu.make_async_copy(src, self.held(j, kind), self.rsem.at[j, kind]).start()
            else:
                pltpu.make_async_copy(src, self.held(j, kind - 8, 1 - c), self.sib_sem(j, kind - 8)).start()

        def put(self, j, src, dst, kind, device):
            sem = self.rsem.at[j, kind] if kind < 8 else self.sib_sem(j, kind - 8)
            remote(src, dst, self.ssem.at[j], sem, device).start()

        def pass_on(self, j, kind_here, kind, device):
            ref = self.held(j, kind_here)
            self.put(j, ref, ref, kind, device)

        def to_sib(self, j, kind):
            self.pass_on(j, kind, 8 + kind, d_sib)

        def wait(self, j, kind):
            ref = self.held(j, kind)
            remote(ref, ref, self.ssem.at[j], self.rsem.at[j, kind], d_sib).wait_recv()

        def wait_sib(self, sem):
            ref = self.buffer.at[0, pl.ds(0, 8 * BLOCK)]
            remote(ref, ref, self.ssem.at[0], sem, d_sib).wait_recv()

        def sent(self, j, count):
            ref = self.buffer.at[j, pl.ds(0, count * BLOCK)]
            remote(ref, ref, self.ssem.at[j], self.rsem.at[j, 0], d_sib).wait_send()

    proj = Gather(wbuf, gsend, grecv, lambda j, kind: gsib.at[j])
    outw = Gather(wobuf, wsend, wrecv, lambda q, kind: wsib.at[group(kind)])

    def source_of(j):
        return ((wk, LANES, 0), (wv, LANES, 0))[j] if j < 2 else (wq, GROUP * LANES, j - 2)

    def cols_of(j, tt):
        source, width, head = source_of(j)
        return source.at[:, pl.ds(al(tt * width + head * LANES, LANES), LANES)]

    def first(j):
        own, dst = cols_of(j, t), proj.held(j, 0)
        proj.put(j, own, dst, 2, d_zp)
        proj.put(j, own, dst, 1, d_zm)
        proj.put(j, cols_of(j, y * 2 + 1 - hi), dst, 3, d_cross)
        proj.put(j, own, dst, 8, d_sib)

    def mid1(j):
        proj.wait(j, 1)
        proj.pass_on(j, 1, 4, d_pair)
        proj.wait(j, 2)
        proj.pass_on(j, 2, 5, d_pair)
        if j % 2 == 0:
            proj.pass_on(j, 1, 6, d_zm)
        else:
            proj.pass_on(j, 2, 6, d_zp)
        proj.to_sib(j, 1)
        proj.to_sib(j, 2)
        proj.wait(j, 3)
        proj.to_sib(j, 3)

    def mid2(j):
        proj.wait(j, 4)
        if j % 2 == 0:
            proj.pass_on(j, 4, 7, d_zm)
        proj.to_sib(j, 4)
        proj.wait(j, 5)
        if j % 2 == 1:
            proj.pass_on(j, 5, 7, d_zp)
        proj.to_sib(j, 5)
        proj.wait(j, 6)
        proj.to_sib(j, 6)

    def fin(j):
        proj.wait(j, 7)
        proj.to_sib(j, 7)
        proj.wait(j, 0)
        proj.wait_sib(gsib.at[j])

    def ow_rows(q, half):
        return wo.at[pl.ds(al(half * 2048 + q * BLOCK, BLOCK), BLOCK), pl.ds(al(y * LANES, LANES), LANES)]

    def ow_load():
        for q in range(QUARTERS):
            @pl.when(c_is_hi)
            def _():
                outw.load(q, ow_rows(q, c), 0)
                outw.load(q, ow_rows(q, 1 - c), 8)
                outw.put(q, ow_rows(q, 1 - c), outw.held(q, 0, 1 - c), 0, d_sib)
                outw.put(q, ow_rows(q, c), outw.held(q, 0), 8, d_sib)

    def ow_first():
        for q in range(QUARTERS):
            outw.wait(q, 0)
            outw.pass_on(q, 0, 2, d_zp)
            outw.pass_on(q, 0, 1, d_zm)
            if q % 2 == 0:
                outw.pass_on(q, 0, 3, d_pair)
            else:
                @pl.when(jnp.logical_not(c_is_hi))
                def _():
                    outw.put(q, ow_rows(q, c), outw.held(q, 0), 3, d_cross)
                    outw.put(q, ow_rows(q, 1 - c), outw.held(q, 0, 1 - c), 3, d_cross_sib)

    def ow_second():
        for q in range(QUARTERS):
            outw.wait(q, 3)
            outw.pass_on(q, 3, 5, d_zp)
            outw.pass_on(q, 3, 4, d_zm)
            outw.to_sib(q, 3)
        for q in range(QUARTERS):
            for kind in (1, 2):
                outw.wait(q, kind)
                outw.to_sib(q, kind)
            if q % 2 == 0:
                outw.pass_on(q, 1, 6, d_zm)
            else:
                outw.pass_on(q, 2, 6, d_zp)

    def ow_third():
        for q in range(QUARTERS):
            for kind in (4, 5):
                outw.wait(q, kind)
                outw.to_sib(q, kind)
            if q % 2 == 0:
                outw.pass_on(q, 4, 7, d_zm)
            else:
                outw.pass_on(q, 5, 7, d_zp)

    def ow_last():
        for q in range(QUARTERS):
            for kind in (6, 7):
                outw.wait(q, kind)
                outw.to_sib(q, kind)

    def ow_ready(i):
        outw.wait_sib(wsib.at[i])

    peer = ((y, hi), (yp, hi), (ym, hi), (y, 1 - hi), (yp, 1 - hi), (ym, 1 - hi), (y2, hi), (y2, 1 - hi))

    class Ring:
        def __init__(self, ssem, rsem, block, seven, across):
            self.ssem, self.rsem, self.block, self.seven, self.across = ssem, rsem, block, seven, across

        def at(self, j, kind):
            return self.block(j, peer[kind][0], peer[kind][1])

        def forward(self, j, kind_here, kind, device):
            ref = self.at(j, kind_here)
            remote(ref, ref, self.ssem.at[j], self.rsem.at[j, kind], device).start()

        def wait(self, j, kind):
            ref = self.at(j, kind)
            remote(ref, ref, self.ssem.at[j], self.rsem.at[j, kind], d_sib).wait_recv()

        def begin(self, j):
            self.forward(j, 0, 2, d_yp)
            self.forward(j, 0, 1, d_ym)
            self.forward(j, 0, 3, d_hi)

        def mid1(self, j):
            up, three = j % 2 == 1, self.across[j] == 3
            self.wait(j, 1)
            if not up:
                self.forward(j, 1, 6, d_ym)
                if three:
                    self.forward(j, 1, 4, d_hi)
            self.wait(j, 2)
            if up:
                self.forward(j, 2, 6, d_yp)
                if three:
                    self.forward(j, 2, 5, d_hi)
            self.wait(j, 3)
            if not (three and up):
                self.forward(j, 3, 5, d_yp)
            if not (three and not up):
                self.forward(j, 3, 4, d_ym)

        def mid2(self, j):
            up, one = j % 2 == 1, self.across[j] == 1
            self.wait(j, 6)
            if not one:
                self.forward(j, 6, 7, d_hi)
            self.wait(j, 4)
            if one and not up:
                self.forward(j, 4, 7, d_ym)
            self.wait(j, 5)
            if one and up:
                self.forward(j, 5, 7, d_yp)

        def fin(self, j):
            self.wait(j, 7)

        def done(self, j):
            remote(self.seven, self.seven, self.ssem.at[j], self.rsem.at[j, 1], d_sib).wait_send()

    def ctx_block(j, yy, hh):
        return ctx.at[yy * 2 + hh, j // 2, pl.ds((j % 2) * HALF, HALF)]

    def out_cols(u, yy, hh):
        zz, ll = place[UNITS[u]]
        return pl.ds(al(((zz * 2 + ll) * 2 + hh) * BLOCK + yy * LANES, LANES), LANES)

    def out_block(j, yy, hh):
        half, u = OUT_ORDER[j]
        return out.at[pl.ds(half * HALF, HALF), out_cols(u, yy, hh)]

    ctx_ring = Ring(csend, crecv, ctx_block, ctx.at[pl.ds(0, 7), 0, pl.ds(0, HALF)], CTX_ACROSS)
    out_ring = Ring(osend, orecv, out_block, out.at[pl.ds(0, HALF), pl.ds(0, 7 * LANES)], OUT_ACROSS)

    def tables():
        def part(i, _):
            rows = pl.ds(al(i * 64, 64), 64)
            token = lax.broadcasted_iota(jnp.int32, (64, LANES), 0) + i * 64
            lane = lax.broadcasted_iota(jnp.int32, (64, LANES), 1)
            mine = jnp.where(lane == token // STEPS, lengths[...].astype(f32), 0.0)
            live = jnp.sum(mine, axis=1, keepdims=True)
            len_ref[rows, :] = jnp.broadcast_to(live, (64, LANES)).astype(jnp.int32)
            angles = (live + (token % STEPS).astype(f32)) * frequency[...]
            cos_ref[rows, :] = jnp.cos(angles)
            sine = jnp.sin(angles)
            sin_ref[rows, :] = jnp.where(lane < HD // 2, -sine, sine)
            return 0

        lax.fori_loop(0, TOKENS // 64, part, 0)

    def norm(i, _):
        rows = pl.ds(al(i * 64, 64), 64)
        width = xn.shape[1]

        def square(k, total):
            v = xn[rows, pl.ds(al(k * 512, 512), 512)].astype(f32)
            v = v * v
            return total + (v[:, :128] + v[:, 128:256]) + (v[:, 256:384] + v[:, 384:])

        total = lax.fori_loop(0, width // 512, square, jnp.zeros((64, 128), f32))
        scale = lax.rsqrt(jnp.sum(total, axis=1, keepdims=True) * (1.0 / width) + epsilon)

        def apply(k, _):
            cols = pl.ds(al(k * 512, 512), 512)
            xn[rows, cols] = (xn[rows, cols].astype(f32) * scale).astype(bf16)
            return 0

        lax.fori_loop(0, width // 512, apply, 0)
        return 0

    def project(p):
        acc[...] = jnp.zeros_like(acc)

        def part(k, _):
            cols = pl.ds(al(k * 1024, 1024), 1024)
            weights = jnp.concatenate([wbuf[2 * p, cols, :], wbuf[2 * p + 1, cols, :]], axis=1)
            acc[...] += jnp.dot(xn[:, cols], weights, preferred_element_type=f32)
            return 0

        lax.fori_loop(0, 8, part, 0)

        def rotated(v):
            return (v * cos_ref[...] + pltpu.roll(v, HD // 2, 1) * sin_ref[...]).astype(bf16)

        if p == 0:
            kn[...] = rotated(acc[:, :HD])
            vn[...] = acc[:, HD:].astype(bf16)
        else:
            qr[2 * p - 2] = rotated(acc[:, :HD])
            qr[2 * p - 1] = rotated(acc[:, HD:])

    scaling = 1.0 / math.sqrt(HD)
    nt = (((1,), (1,)), ((), ()))

    def attend(p, i):
        fresh = slice(i * 128, (i + 1) * 128)
        token = lax.broadcasted_iota(jnp.int32, (32, 1), 0) % 16
        row = token // STEPS
        scores = []
        for b in range(8):
            tok = slice(i * 128 + b * 16, i * 128 + (b + 1) * 16)
            q = jnp.concatenate([qr[2 * p, tok, :], qr[2 * p + 1, tok, :]], axis=0)
            keys = kc[(i * 8 + b) * 512:(i * 8 + b + 1) * 512, :]
            older = lax.dot_general(q, keys, nt, preferred_element_type=f32) * scaling
            recent = lax.dot_general(q, kn[fresh, :], nt, preferred_element_type=f32) * scaling
            scores.append((older, recent))
        for b in range(8):
            older, recent = scores[b]
            live = len_ref[i * 128 + b * 16:i * 128 + (b + 1) * 16, :1]
            live = jnp.concatenate([live, live], axis=0)
            lane = lax.broadcasted_iota(jnp.int32, older.shape, 1)
            older = jnp.where((lane >= row * 128) & (lane < row * 128 + live), older, masked)
            lane = lax.broadcasted_iota(jnp.int32, recent.shape, 1) - b * 16
            recent = jnp.where((lane >= row * STEPS) & (lane <= token), recent, masked)
            scores[b] = older, recent
        highest = [
            jnp.maximum(jnp.max(older, axis=1, keepdims=True), jnp.max(recent, axis=1, keepdims=True))
            for older, recent in scores
        ]
        scores = [(jnp.exp(older - h), jnp.exp(recent - h)) for (older, recent), h in zip(scores, highest)]
        inverse = [
            1.0 / (jnp.sum(older, axis=1, keepdims=True) + jnp.sum(recent, axis=1, keepdims=True))
            for older, recent in scores
        ]
        mixes = []
        for b in range(8):
            older, recent = scores[b]
            values = vc[(i * 8 + b) * 512:(i * 8 + b + 1) * 512, :]
            mix = jnp.dot((older * inverse[b]).astype(bf16), values, preferred_element_type=f32)
            mix += jnp.dot((recent * inverse[b]).astype(bf16), vn[fresh, :], preferred_element_type=f32)
            mixes.append(mix.astype(bf16))
        for b in range(8):
            tok = slice(i * 128 + b * 16, i * 128 + (b + 1) * 16)
            ctx[t, p, tok, :] = jnp.concatenate([mixes[b][:16], mixes[b][16:]], axis=1)

    def out_units(half, u):
        rows = slice(half * HALF, (half + 1) * HALF)
        part_sum = acc.at[:HALF]
        part_sum[...] = jnp.zeros_like(part_sum)
        slots = [(place[UNITS[u + i]][0] * 2 + place[UNITS[u + i]][1]) * 2 for i in range(2)]

        def part(i, _):
            def weights(tt):
                side = tt // 4
                pieces = [wobuf[tt % 4, pl.ds(al((slot + side) * BLOCK, BLOCK), BLOCK), :] for slot in slots]
                return jnp.concatenate(pieces, axis=1)

            left = jnp.concatenate([ctx[2 * i + k // 2, k % 2, rows, :] for k in range(4)], axis=1)
            right = jnp.concatenate([weights(2 * i), weights(2 * i + 1)], axis=0)
            part_sum[...] += jnp.dot(left, right, preferred_element_type=f32)
            return 0

        lax.fori_loop(0, TP // 2, part, 0)
        for i in range(2):
            out[rows, out_cols(u + i, y, hi)] = part_sum[:, i * LANES:(i + 1) * LANES].astype(bf16)

    xload = pltpu.make_async_copy(hidden.reshape(TOKENS, hidden.shape[2]), xn, local_sem.at[0])
    kload = pltpu.make_async_copy(kcache, kc, local_sem.at[1])
    vload = pltpu.make_async_copy(vcache, vc, local_sem.at[2])
    barrier = pltpu.get_barrier_semaphore()
    partners = (d_hi, d_zp, d_zm, d_yp, d_ym, d_pair, d_cross, d_cross_sib, d_sib)
    for device in partners:
        pl.semaphore_signal(barrier, inc=1, device_id=device, device_id_type=MESH)
    for j in range(JOBS):
        proj.load(j, cols_of(j, t), 0)
    xload.start()
    kload.start()
    vload.start()
    tables()
    pl.semaphore_wait(barrier, len(partners))
    first(0)
    first(1)
    xload.wait()
    lax.fori_loop(0, TOKENS // 64, norm, 0)
    for j in range(4):
        mid1(j)
        first(j + 2)
        if j >= 1:
            mid2(j - 1)
        if j >= 2:
            fin(j - 2)
    project(0)
    mid1(4)
    mid2(3)
    fin(2)
    ow_load()
    mid1(5)
    mid2(4)
    fin(3)
    project(1)
    kload.wait()
    vload.wait()
    mid2(5)
    attend(0, 0)
    attend(0, 1)
    ctx_ring.begin(0)
    fin(4)
    attend(0, 2)
    attend(0, 3)
    ctx_ring.begin(1)
    ctx_ring.mid1(0)
    fin(5)
    ow_first()
    ctx_ring.mid1(1)
    project(2)
    ctx_ring.mid2(0)
    attend(1, 0)
    attend(1, 1)
    ctx_ring.begin(2)
    ctx_ring.mid2(1)
    attend(1, 2)
    attend(1, 3)
    ctx_ring.begin(3)
    ctx_ring.mid1(2)
    ow_second()
    ctx_ring.mid1(3)
    ctx_ring.mid2(2)
    ctx_ring.fin(0)
    ctx_ring.fin(2)
    ctx_ring.mid2(3)
    for j in range(OUT_JOBS):
        if j == 4:
            ctx_ring.fin(1)
            ctx_ring.fin(3)
            ow_third()
        if j == 8:
            ow_last()
        if j % 2 == 0:
            half, u = OUT_ORDER[j]
            if half == 0:
                ow_ready(u // 2)
            out_units(half, u)
        out_ring.begin(j)
        if j >= 2:
            out_ring.mid1(j - 2)
        if j >= 4:
            out_ring.mid2(j - 4)
    for j in range(JOBS):
        proj.sent(j, 15)
    out_ring.mid2(OUT_JOBS - 4)
    out_ring.mid1(OUT_JOBS - 2)
    for q in range(QUARTERS):
        if q % 2 == 1:
            outw.sent(q, 15)
        else:
            @pl.when(c_is_hi)
            def _():
                outw.sent(q, 16)

            @pl.when(jnp.logical_not(c_is_hi))
            def _():
                outw.sent(q, 14)
    out_ring.mid2(OUT_JOBS - 3)
    out_ring.mid1(OUT_JOBS - 1)
    for j in range(4):
        ctx_ring.done(j)
    out_ring.mid2(OUT_JOBS - 2)
    out_ring.mid2(OUT_JOBS - 1)
    for j in range(OUT_JOBS):
        out_ring.fin(j)
    for j in range(OUT_JOBS):
        out_ring.done(j)


def place_result(held, out, sem):
    flat = out.reshape(held.shape)
    copies = []
    for i in range(4):
        rows = pl.ds(i * 128, 128)
        copies.append(pltpu.make_async_copy(held.at[rows], flat.at[rows], sem.at[i]))
        copies[-1].start()
    for copy in copies:
        copy.wait()


def body(
    hidden_in, lengths, key_cache, value_cache, query_weight, key_weight, value_weight, out_weight
):
    row_count, step_count, width = hidden_in.shape
    slots = key_cache.shape[1]
    frequency = np.tile(rope_base ** (-(np.arange(HD // 2) * 2.0) / HD), 2).astype(np.float32)[None, :]
    hbm = pl.BlockSpec(memory_space=pl.ANY)
    vmem = pl.BlockSpec(memory_space=pltpu.VMEM)
    dma = pltpu.SemaphoreType.DMA
    result = pl.pallas_call(
        layer_kernel,
        out_shape=pltpu.VMEM((TOKENS, width), bf16),
        in_specs=[hbm] * 7 + [vmem] * 2,
        out_specs=vmem,
        scratch_shapes=[
            pltpu.VMEM((JOBS, width, LANES), bf16),
            pltpu.VMEM((QUARTERS, width, LANES), bf16),
            pltpu.VMEM((TOKENS, width), bf16),
            pltpu.VMEM((row_count * slots, HD), bf16),
            pltpu.VMEM((row_count * slots, HD), bf16),
            pltpu.VMEM((GROUP, TOKENS, HD), bf16),
            pltpu.VMEM((TOKENS, HD), bf16),
            pltpu.VMEM((TOKENS, HD), bf16),
            pltpu.VMEM((TP, 2, TOKENS, 2 * HD), bf16),
            pltpu.VMEM((TOKENS, 2 * LANES), f32),
            pltpu.VMEM((TOKENS, LANES), f32),
            pltpu.VMEM((TOKENS, LANES), f32),
            pltpu.VMEM((TOKENS, LANES), jnp.int32),
            dma((JOBS,)),
            dma((JOBS, 8)),
            dma((JOBS,)),
            dma((QUARTERS,)),
            dma((QUARTERS, 8)),
            dma((4,)),
            dma((4,)),
            dma((4, 8)),
            dma((OUT_JOBS,)),
            dma((OUT_JOBS, 8)),
            dma((3,)),
        ],
        compiler_params=pltpu.CompilerParams(
            collective_id=0, has_side_effects=True, vmem_limit_bytes=50 * 1024 * 1024
        ),
        name="attention_layer",
    )(
        hidden_in,
        key_cache.reshape(row_count * slots, HD),
        value_cache.reshape(row_count * slots, HD),
        query_weight, key_weight, value_weight, out_weight,
        lengths.reshape(1, row_count), jnp.asarray(frequency),
    )
    return pl.pallas_call(
        place_result,
        out_shape=jax.ShapeDtypeStruct(hidden_in.shape, bf16),
        in_specs=[vmem],
        out_specs=hbm,
        scratch_shapes=[dma((4,))],
        compiler_params=pltpu.CompilerParams(vmem_limit_bytes=1024 * 1024),
        name="place_result",
    )(result)


def solution(mesh):
    return jax.shard_map(
        body,
        mesh=mesh,
        in_specs=(
            P("fsdp", None, None),
            P("fsdp"),
            P("fsdp", None, "tp"),
            P("fsdp", None, "tp"),
            P("fsdp", None),
            P("fsdp", None),
            P("fsdp", None),
            P(None, "fsdp"),
        ),
        out_specs=P("fsdp", None, None),
        check_vma=False,
    )
```

```python
import math

import jax
import jax.numpy as jnp
import numpy as np
from jax import lax
from jax.experimental import pallas as pl
from jax.experimental.pallas import tpu as pltpu
from jax.sharding import PartitionSpec as P

HD = 128
STEPS = 4
GROUP = 4
LANES = 128
rope_base = 1000000.0
epsilon = 1e-06
masked = -1e30

MESH = pl.DeviceIdType.MESH
f32 = jnp.float32
bf16 = jnp.bfloat16

JOBS = 6
QUARTERS = 4
BLOCK = 512
TOKENS = 512
HALF = TOKENS // 2
TP = 8
UNITS = (0, 3, 1, 2, 4, 5, 6, 7)
OUT_PAIRS = ((0, 0), (0, 2), (1, 0), (1, 2), (0, 4), (1, 4), (0, 6), (1, 6))
OUT_ORDER = tuple((half, u + i) for half, u in OUT_PAIRS for i in range(2))
OUT_JOBS = len(OUT_ORDER)
CTX_JOBS = 2 * GROUP
CTX_ACROSS = (2,) * CTX_JOBS
OUT_ACROSS = (2, 2, 3) * 5 + (2,)


def al(x, m):
    return pl.multiple_of(x, m)


def layer_kernel(
    hidden, kcache, vcache, wq, wk, wv, wo, lengths, frequency,
    out,
    wbuf, wobuf, xn, kc, vc, qr, kn, vn, ctx, acc, cos_ref, sin_ref, len_ref,
    gsend, grecv, gsib, wsend, wrecv, wsib, csend, crecv, osend, orecv, local_sem,
):
    f, t = lax.axis_index("fsdp"), lax.axis_index("tp")
    z, lo, c = f // 4, (f // 2) % 2, f % 2
    y, hi = t // 2, t % 2
    c_is_hi = c == hi

    def dev(zz=z, ll=lo, cc=c, yy=y, hh=hi):
        return (zz * 4 + ll * 2 + cc, yy * 2 + hh)

    zp, zm, z2 = (z + 1) % 4, (z + 3) % 4, (z + 2) % 4
    yp, ym, y2 = (y + 1) % 4, (y + 3) % 4, (y + 2) % 4
    d_zp, d_zm = dev(zz=zp), dev(zz=zm)
    d_yp, d_ym = dev(yy=yp), dev(yy=ym)
    d_pair, d_hi, d_sib = dev(ll=1 - lo), dev(hh=1 - hi), dev(cc=1 - c)
    d_cross = dev(ll=1 - lo, hh=1 - hi)
    d_cross_sib = dev(ll=1 - lo, hh=1 - hi, cc=1 - c)

    def remote(src, dst, ssem, rsem, device):
        return pltpu.make_async_remote_copy(
            src_ref=src, dst_ref=dst, send_sem=ssem, recv_sem=rsem, device_id=device, device_id_type=MESH
        )

    place = ((z, lo), (zp, lo), (zm, lo), (z, 1 - lo), (zp, 1 - lo), (zm, 1 - lo), (z2, lo), (z2, 1 - lo))

    def group(kind):
        return (0, 1, 1, 0, 2, 2, 3, 3)[kind]

    class Gather:
        def __init__(self, buffer, ssem, rsem, sib_sem):
            self.buffer, self.ssem, self.rsem, self.sib_sem = buffer, ssem, rsem, sib_sem

        def held(self, j, kind, cc=c):
            zz, ll = place[kind]
            return self.buffer.at[j, pl.ds(al(((zz * 2 + ll) * 2 + cc) * BLOCK, BLOCK), BLOCK)]

        def load(self, j, src, kind):
            if kind < 8:
                pltpu.make_async_copy(src, self.held(j, kind), self.rsem.at[j, kind]).start()
            else:
                pltpu.make_async_copy(src, self.held(j, kind - 8, 1 - c), self.sib_sem(j, kind - 8)).start()

        def put(self, j, src, dst, kind, device):
            sem = self.rsem.at[j, kind] if kind < 8 else self.sib_sem(j, kind - 8)
            remote(src, dst, self.ssem.at[j], sem, device).start()

        def pass_on(self, j, kind_here, kind, device):
            ref = self.held(j, kind_here)
            self.put(j, ref, ref, kind, device)

        def to_sib(self, j, kind):
            self.pass_on(j, kind, 8 + kind, d_sib)

        def wait(self, j, kind):
            ref = self.held(j, kind)
            remote(ref, ref, self.ssem.at[j], self.rsem.at[j, kind], d_sib).wait_recv()

        def wait_sib(self, sem):
            ref = self.buffer.at[0, pl.ds(0, 8 * BLOCK)]
            remote(ref, ref, self.ssem.at[0], sem, d_sib).wait_recv()

        def sent(self, j, count):
            ref = self.buffer.at[j, pl.ds(0, count * BLOCK)]
            remote(ref, ref, self.ssem.at[j], self.rsem.at[j, 0], d_sib).wait_send()

    proj = Gather(wbuf, gsend, grecv, lambda j, kind: gsib.at[j])
    outw = Gather(wobuf, wsend, wrecv, lambda q, kind: wsib.at[group(kind)])

    def source_of(j):
        return ((wk, LANES, 0), (wv, LANES, 0))[j] if j < 2 else (wq, GROUP * LANES, j - 2)

    def cols_of(j, tt):
        source, width, head = source_of(j)
        return source.at[:, pl.ds(al(tt * width + head * LANES, LANES), LANES)]

    def first(j):
        own, dst = cols_of(j, t), proj.held(j, 0)
        proj.put(j, own, dst, 2, d_zp)
        proj.put(j, own, dst, 1, d_zm)
        proj.put(j, cols_of(j, y * 2 + 1 - hi), dst, 3, d_cross)
        proj.put(j, own, dst, 8, d_sib)

    def mid1(j):
        proj.wait(j, 1)
        proj.pass_on(j, 1, 4, d_pair)
        proj.wait(j, 2)
        proj.pass_on(j, 2, 5, d_pair)
        if j % 2 == 0:
            proj.pass_on(j, 1, 6, d_zm)
        else:
            proj.pass_on(j, 2, 6, d_zp)
        proj.to_sib(j, 1)
        proj.to_sib(j, 2)
        proj.wait(j, 3)
        proj.to_sib(j, 3)

    def mid2(j):
        proj.wait(j, 4)
        if j % 2 == 0:
            proj.pass_on(j, 4, 7, d_zm)
        proj.to_sib(j, 4)
        proj.wait(j, 5)
        if j % 2 == 1:
            proj.pass_on(j, 5, 7, d_zp)
        proj.to_sib(j, 5)
        proj.wait(j, 6)
        proj.to_sib(j, 6)

    def fin(j):
        proj.wait(j, 7)
        proj.to_sib(j, 7)
        proj.wait(j, 0)
        proj.wait_sib(gsib.at[j])

    def ow_rows(q, half):
        return wo.at[pl.ds(al(half * 2048 + q * BLOCK, BLOCK), BLOCK), pl.ds(al(y * LANES, LANES), LANES)]

    def ow_load():
        for q in range(QUARTERS):
            @pl.when(c_is_hi)
            def _():
                outw.load(q, ow_rows(q, c), 0)
                outw.load(q, ow_rows(q, 1 - c), 8)
                outw.put(q, ow_rows(q, 1 - c), outw.held(q, 0, 1 - c), 0, d_sib)
                outw.put(q, ow_rows(q, c), outw.held(q, 0), 8, d_sib)

    def ow_first():
        for q in range(QUARTERS):
            outw.wait(q, 0)
            outw.pass_on(q, 0, 2, d_zp)
            outw.pass_on(q, 0, 1, d_zm)
            if q % 2 == 0:
                outw.pass_on(q, 0, 3, d_pair)
            else:
                @pl.when(jnp.logical_not(c_is_hi))
                def _():
                    outw.put(q, ow_rows(q, c), outw.held(q, 0), 3, d_cross)
                    outw.put(q, ow_rows(q, 1 - c), outw.held(q, 0, 1 - c), 3, d_cross_sib)

    def ow_second():
        for q in range(QUARTERS):
            outw.wait(q, 3)
            outw.pass_on(q, 3, 5, d_zp)
            outw.pass_on(q, 3, 4, d_zm)
            outw.to_sib(q, 3)
        for q in range(QUARTERS):
            for kind in (1, 2):
                outw.wait(q, kind)
                outw.to_sib(q, kind)
            if q % 2 == 0:
                outw.pass_on(q, 1, 6, d_zm)
            else:
                outw.pass_on(q, 2, 6, d_zp)

    def ow_third():
        for q in range(QUARTERS):
            for kind in (4, 5):
                outw.wait(q, kind)
                outw.to_sib(q, kind)
            if q % 2 == 0:
                outw.pass_on(q, 4, 7, d_zm)
            else:
                outw.pass_on(q, 5, 7, d_zp)

    def ow_last():
        for q in range(QUARTERS):
            for kind in (6, 7):
                outw.wait(q, kind)
                outw.to_sib(q, kind)

    def ow_ready(i):
        outw.wait_sib(wsib.at[i])

    peer = ((y, hi), (yp, hi), (ym, hi), (y, 1 - hi), (yp, 1 - hi), (ym, 1 - hi), (y2, hi), (y2, 1 - hi))

    class Ring:
        def __init__(self, ssem, rsem, block, seven, across):
            self.ssem, self.rsem, self.block, self.seven, self.across = ssem, rsem, block, seven, across

        def at(self, j, kind):
            return self.block(j, peer[kind][0], peer[kind][1])

        def forward(self, j, kind_here, kind, device):
            ref = self.at(j, kind_here)
            remote(ref, ref, self.ssem.at[j], self.rsem.at[j, kind], device).start()

        def wait(self, j, kind):
            ref = self.at(j, kind)
            remote(ref, ref, self.ssem.at[j], self.rsem.at[j, kind], d_sib).wait_recv()

        def begin(self, j):
            self.forward(j, 0, 2, d_yp)
            self.forward(j, 0, 1, d_ym)
            self.forward(j, 0, 3, d_hi)

        def mid1(self, j):
            up, three = j % 2 == 1, self.across[j] == 3
            self.wait(j, 1)
            if not up:
                self.forward(j, 1, 6, d_ym)
                if three:
                    self.forward(j, 1, 4, d_hi)
            self.wait(j, 2)
            if up:
                self.forward(j, 2, 6, d_yp)
                if three:
                    self.forward(j, 2, 5, d_hi)
            self.wait(j, 3)
            if not (three and up):
                self.forward(j, 3, 5, d_yp)
            if not (three and not up):
                self.forward(j, 3, 4, d_ym)

        def mid2(self, j):
            up, one = j % 2 == 1, self.across[j] == 1
            self.wait(j, 6)
            if not one:
                self.forward(j, 6, 7, d_hi)
            self.wait(j, 4)
            if one and not up:
                self.forward(j, 4, 7, d_ym)
            self.wait(j, 5)
            if one and up:
                self.forward(j, 5, 7, d_yp)

        def fin(self, j):
            self.wait(j, 7)

        def done(self, j):
            remote(self.seven, self.seven, self.ssem.at[j], self.rsem.at[j, 1], d_sib).wait_send()

    def ctx_block(j, yy, hh):
        return ctx.at[yy * 2 + hh, j // 2, pl.ds((j % 2) * HALF, HALF)]

    def out_cols(u, yy, hh):
        zz, ll = place[UNITS[u]]
        return pl.ds(al(((zz * 2 + ll) * 2 + hh) * BLOCK + yy * LANES, LANES), LANES)

    def out_block(j, yy, hh):
        half, u = OUT_ORDER[j]
        return out.at[pl.ds(half * HALF, HALF), out_cols(u, yy, hh)]

    ctx_ring = Ring(csend, crecv, ctx_block, ctx.at[pl.ds(0, 7), 0, pl.ds(0, HALF)], CTX_ACROSS)
    out_ring = Ring(osend, orecv, out_block, out.at[pl.ds(0, HALF), pl.ds(0, 7 * LANES)], OUT_ACROSS)

    def tables():
        def part(i, _):
            rows = pl.ds(al(i * 64, 64), 64)
            token = lax.broadcasted_iota(jnp.int32, (64, LANES), 0) + i * 64
            lane = lax.broadcasted_iota(jnp.int32, (64, LANES), 1)
            mine = jnp.where(lane == token // STEPS, lengths[...].astype(f32), 0.0)
            live = jnp.sum(mine, axis=1, keepdims=True)
            len_ref[rows, :] = jnp.broadcast_to(live, (64, LANES)).astype(jnp.int32)
            angles = (live + (token % STEPS).astype(f32)) * frequency[...]
            cos_ref[rows, :] = jnp.cos(angles)
            sine = jnp.sin(angles)
            sin_ref[rows, :] = jnp.where(lane < HD // 2, -sine, sine)
            return 0

        lax.fori_loop(0, TOKENS // 64, part, 0)

    def norm(i, _):
        rows = pl.ds(al(i * 64, 64), 64)
        width = xn.shape[1]

        def square(k, total):
            v = xn[rows, pl.ds(al(k * 512, 512), 512)].astype(f32)
            v = v * v
            return total + (v[:, :128] + v[:, 128:256]) + (v[:, 256:384] + v[:, 384:])

        total = lax.fori_loop(0, width // 512, square, jnp.zeros((64, 128), f32))
        scale = lax.rsqrt(jnp.sum(total, axis=1, keepdims=True) * (1.0 / width) + epsilon)

        def apply(k, _):
            cols = pl.ds(al(k * 512, 512), 512)
            xn[rows, cols] = (xn[rows, cols].astype(f32) * scale).astype(bf16)
            return 0

        lax.fori_loop(0, width // 512, apply, 0)
        return 0

    def rotated(v):
        return (v * cos_ref[...] + pltpu.roll(v, HD // 2, 1) * sin_ref[...]).astype(bf16)

    def product(total, depth, weights):
        total[...] = jnp.zeros_like(total)

        def part(k, _):
            rows = pl.ds(al(k * depth, depth), depth)
            total[...] += jnp.dot(xn[:, rows], weights(rows), preferred_element_type=f32)
            return 0

        lax.fori_loop(0, xn.shape[1] // depth, part, 0)

    def project_kv():
        product(acc, 1024, lambda rows: jnp.concatenate([wbuf[0, rows, :], wbuf[1, rows, :]], axis=1))
        kn[...] = rotated(acc[:, :HD])
        vn[...] = acc[:, HD:].astype(bf16)

    def project_q(h):
        product(acc.at[:, :HD], 2048, lambda rows: wbuf[2 + h, rows, :])
        qr[h] = rotated(acc[:, :HD])

    scaling = 1.0 / math.sqrt(HD)
    nt = (((1,), (1,)), ((), ()))

    def attend(h, i):
        fresh = slice(i * 128, (i + 1) * 128)
        token = lax.broadcasted_iota(jnp.int32, (16, 1), 0)
        row = token // STEPS
        scores = []
        for b in range(8):
            tok = slice(i * 128 + b * 16, i * 128 + (b + 1) * 16)
            q = qr[h, tok, :]
            keys = kc[(i * 8 + b) * 512:(i * 8 + b + 1) * 512, :]
            older = lax.dot_general(q, keys, nt, preferred_element_type=f32) * scaling
            recent = lax.dot_general(q, kn[fresh, :], nt, preferred_element_type=f32) * scaling
            scores.append((older, recent))
        for b in range(8):
            older, recent = scores[b]
            live = len_ref[i * 128 + b * 16:i * 128 + (b + 1) * 16, :1]
            lane = lax.broadcasted_iota(jnp.int32, older.shape, 1)
            older = jnp.where((lane >= row * 128) & (lane < row * 128 + live), older, masked)
            lane = lax.broadcasted_iota(jnp.int32, recent.shape, 1) - b * 16
            recent = jnp.where((lane >= row * STEPS) & (lane <= token), recent, masked)
            scores[b] = older, recent
        tops = [
            jnp.maximum(jnp.max(older, axis=1, keepdims=True), jnp.max(recent, axis=1, keepdims=True))
            for older, recent in scores
        ]
        scores = [(jnp.exp(older - h), jnp.exp(recent - h)) for (older, recent), h in zip(scores, tops)]
        inverse = [
            1.0 / (jnp.sum(older, axis=1, keepdims=True) + jnp.sum(recent, axis=1, keepdims=True))
            for older, recent in scores
        ]
        mixes = []
        for b in range(8):
            older, recent = scores[b]
            values = vc[(i * 8 + b) * 512:(i * 8 + b + 1) * 512, :]
            mix = jnp.dot((older * inverse[b]).astype(bf16), values, preferred_element_type=f32)
            mix += jnp.dot((recent * inverse[b]).astype(bf16), vn[fresh, :], preferred_element_type=f32)
            mixes.append(mix.astype(bf16))
        for b in range(8):
            tok = slice(i * 128 + b * 16, i * 128 + (b + 1) * 16)
            ctx[t, h, tok, :] = mixes[b]

    def out_units(half, u):
        rows = slice(half * HALF, (half + 1) * HALF)
        part_sum = acc.at[:HALF]
        part_sum[...] = jnp.zeros_like(part_sum)
        slots = [(place[UNITS[u + i]][0] * 2 + place[UNITS[u + i]][1]) * 2 for i in range(2)]

        def part(i, _):
            def weights(tt):
                side = tt // 4
                pieces = [wobuf[tt % 4, pl.ds(al((slot + side) * BLOCK, BLOCK), BLOCK), :] for slot in slots]
                return jnp.concatenate(pieces, axis=1)

            left = jnp.concatenate([ctx[2 * i + k // 4, k % 4, rows, :] for k in range(8)], axis=1)
            right = jnp.concatenate([weights(2 * i), weights(2 * i + 1)], axis=0)
            part_sum[...] += jnp.dot(left, right, preferred_element_type=f32)
            return 0

        lax.fori_loop(0, TP // 2, part, 0)
        for i in range(2):
            out[rows, out_cols(u + i, y, hi)] = part_sum[:, i * LANES:(i + 1) * LANES].astype(bf16)

    xload = pltpu.make_async_copy(hidden.reshape(TOKENS, hidden.shape[2]), xn, local_sem.at[0])
    kload = pltpu.make_async_copy(kcache, kc, local_sem.at[1])
    vload = pltpu.make_async_copy(vcache, vc, local_sem.at[2])
    barrier = pltpu.get_barrier_semaphore()
    partners = (d_hi, d_zp, d_zm, d_yp, d_ym, d_pair, d_cross, d_cross_sib, d_sib)
    for device in partners:
        pl.semaphore_signal(barrier, inc=1, device_id=device, device_id_type=MESH)
    for j in range(JOBS):
        proj.load(j, cols_of(j, t), 0)
    xload.start()
    kload.start()
    vload.start()
    tables()
    pl.semaphore_wait(barrier, len(partners))
    first(0)
    first(1)
    xload.wait()
    lax.fori_loop(0, TOKENS // 64, norm, 0)
    for j in range(4):
        mid1(j)
        first(j + 2)
        if j >= 1:
            mid2(j - 1)
        if j >= 2:
            fin(j - 2)
    project_kv()
    mid1(4)
    mid2(3)
    fin(2)
    ow_load()
    project_q(0)
    kload.wait()
    vload.wait()
    mid1(5)
    attend(0, 0)
    attend(0, 1)
    ctx_ring.begin(0)
    mid2(4)
    fin(3)
    attend(0, 2)
    attend(0, 3)
    ctx_ring.begin(1)
    project_q(1)
    mid2(5)
    fin(4)
    ctx_ring.mid1(0)
    attend(1, 0)
    attend(1, 1)
    ctx_ring.begin(2)
    ctx_ring.mid1(1)
    attend(1, 2)
    attend(1, 3)
    ctx_ring.begin(3)
    ctx_ring.mid2(0)
    fin(5)
    ow_first()
    project_q(2)
    ctx_ring.mid1(2)
    attend(2, 0)
    attend(2, 1)
    ctx_ring.begin(4)
    ctx_ring.mid1(3)
    ctx_ring.mid2(1)
    attend(2, 2)
    attend(2, 3)
    ctx_ring.begin(5)
    project_q(3)
    ctx_ring.mid1(4)
    ctx_ring.mid2(2)
    attend(3, 0)
    attend(3, 1)
    ctx_ring.begin(6)
    ctx_ring.mid1(5)
    ctx_ring.mid2(3)
    attend(3, 2)
    attend(3, 3)
    ctx_ring.begin(7)
    ctx_ring.mid2(4)
    ctx_ring.mid1(6)
    ctx_ring.mid2(5)
    ctx_ring.mid1(7)
    ow_second()
    ctx_ring.mid2(6)
    ctx_ring.fin(0)
    ctx_ring.fin(2)
    ctx_ring.fin(4)
    ctx_ring.fin(6)
    ctx_ring.mid2(7)
    for j in range(OUT_JOBS):
        if j == 4:
            for k in range(1, CTX_JOBS, 2):
                ctx_ring.fin(k)
            ow_third()
        if j == 8:
            ow_last()
        if j % 2 == 0:
            half, u = OUT_ORDER[j]
            if half == 0:
                ow_ready(u // 2)
            out_units(half, u)
        out_ring.begin(j)
        if j >= 2:
            out_ring.mid1(j - 2)
        if j >= 4:
            out_ring.mid2(j - 4)
    for j in range(JOBS):
        proj.sent(j, 15)
    out_ring.mid2(OUT_JOBS - 4)
    out_ring.mid1(OUT_JOBS - 2)
    for q in range(QUARTERS):
        if q % 2 == 1:
            outw.sent(q, 15)
        else:
            @pl.when(c_is_hi)
            def _():
                outw.sent(q, 16)

            @pl.when(jnp.logical_not(c_is_hi))
            def _():
                outw.sent(q, 14)
    out_ring.mid2(OUT_JOBS - 3)
    out_ring.mid1(OUT_JOBS - 1)
    for j in range(CTX_JOBS):
        ctx_ring.done(j)
    out_ring.mid2(OUT_JOBS - 2)
    out_ring.mid2(OUT_JOBS - 1)
    for j in range(OUT_JOBS):
        out_ring.fin(j)
    for j in range(OUT_JOBS):
        out_ring.done(j)


def place_result(held, out, sem):
    flat = out.reshape(held.shape)
    copies = []
    for i in range(4):
        rows = pl.ds(i * 128, 128)
        copies.append(pltpu.make_async_copy(held.at[rows], flat.at[rows], sem.at[i]))
        copies[-1].start()
    for copy in copies:
        copy.wait()


def body(
    hidden_in, lengths, key_cache, value_cache, query_weight, key_weight, value_weight, out_weight
):
    row_count, step_count, width = hidden_in.shape
    slots = key_cache.shape[1]
    frequency = np.tile(rope_base ** (-(np.arange(HD // 2) * 2.0) / HD), 2).astype(np.float32)[None, :]
    hbm = pl.BlockSpec(memory_space=pl.ANY)
    vmem = pl.BlockSpec(memory_space=pltpu.VMEM)
    dma = pltpu.SemaphoreType.DMA
    result = pl.pallas_call(
        layer_kernel,
        out_shape=pltpu.VMEM((TOKENS, width), bf16),
        in_specs=[hbm] * 7 + [vmem] * 2,
        out_specs=vmem,
        scratch_shapes=[
            pltpu.VMEM((JOBS, width, LANES), bf16),
            pltpu.VMEM((QUARTERS, width, LANES), bf16),
            pltpu.VMEM((TOKENS, width), bf16),
            pltpu.VMEM((row_count * slots, HD), bf16),
            pltpu.VMEM((row_count * slots, HD), bf16),
            pltpu.VMEM((GROUP, TOKENS, HD), bf16),
            pltpu.VMEM((TOKENS, HD), bf16),
            pltpu.VMEM((TOKENS, HD), bf16),
            pltpu.VMEM((TP, GROUP, TOKENS, HD), bf16),
            pltpu.VMEM((TOKENS, 2 * LANES), f32),
            pltpu.VMEM((TOKENS, LANES), f32),
            pltpu.VMEM((TOKENS, LANES), f32),
            pltpu.VMEM((TOKENS, LANES), jnp.int32),
            dma((JOBS,)),
            dma((JOBS, 8)),
            dma((JOBS,)),
            dma((QUARTERS,)),
            dma((QUARTERS, 8)),
            dma((4,)),
            dma((CTX_JOBS,)),
            dma((CTX_JOBS, 8)),
            dma((OUT_JOBS,)),
            dma((OUT_JOBS, 8)),
            dma((3,)),
        ],
        compiler_params=pltpu.CompilerParams(
            collective_id=0, has_side_effects=True, vmem_limit_bytes=50 * 1024 * 1024
        ),
        name="attention_layer",
    )(
        hidden_in,
        key_cache.reshape(row_count * slots, HD),
        value_cache.reshape(row_count * slots, HD),
        query_weight, key_weight, value_weight, out_weight,
        lengths.reshape(1, row_count), jnp.asarray(frequency),
    )
    return pl.pallas_call(
        place_result,
        out_shape=jax.ShapeDtypeStruct(hidden_in.shape, bf16),
        in_specs=[vmem],
        out_specs=hbm,
        scratch_shapes=[dma((4,))],
        compiler_params=pltpu.CompilerParams(vmem_limit_bytes=1024 * 1024),
        name="place_result",
    )(result)


def solution(mesh):
    return jax.shard_map(
        body,
        mesh=mesh,
        in_specs=(
            P("fsdp", None, None),
            P("fsdp"),
            P("fsdp", None, "tp"),
            P("fsdp", None, "tp"),
            P("fsdp", None),
            P("fsdp", None),
            P("fsdp", None),
            P(None, "fsdp"),
        ),
        out_specs=P("fsdp", None, None),
        check_vma=False,
    )
```
